512 devices in a mesh: cp: 128 (over z_lo, y, x, core), tp: 4 (over z_hi).
Axes of the slice: x: 4, y: 4, z: 16 (z_hi: 4, z_lo: 4; z = z_hi * 4 + z_lo), core: 2. Of those that a mesh axis runs over, the one named last changes fastest.
Arguments:
- queries: bfloat16 [2, 128, 256, 4096], P(None, 'cp', None, 'tp'), may hold values from -40 to 40
- keys: bfloat16 [2, 128, 256, 512], P(None, 'cp', 'tp'), may hold values from -8 to 8
- values: bfloat16 [2, 128, 256, 512], P(None, 'cp', 'tp'), may hold values from -6 to 6
- out_grad: bfloat16 [2, 128, 256, 4096], P(None, 'cp', None, 'tp'), may hold values from -6 to 6
- doc_lengths: int32 [256], replicated, may hold values from 1 to 512, 65536 in all
Outputs:
- attn_out: bfloat16 [2, 128, 256, 4096], P(None, 'cp', None, 'tp')
- q_grad: bfloat16 [2, 128, 256, 4096], P(None, 'cp', None, 'tp')
- k_grad: bfloat16 [2, 128, 256, 512], P(None, 'cp', 'tp')
- v_grad: bfloat16 [2, 128, 256, 512], P(None, 'cp', 'tp')
The draws below stay inside these ranges and needn't reach their ends.
Inputs may be any that keep to these rules, and one draw needn't show every extreme that they name: `doc_lengths`: the documents lie in order and tile the whole sequence; one of them is exactly 512 tokens long.
All inputs are finite; a program needn't handle non-finite values.
Results may differ from the reference program's by a relative error of at most 0.012.
The reference program's roundings to bfloat16 on the way (of `probs_low` and `dscores`) count: a program that leaves them out, or rounds other values in their place, can miss the bound.
Values may be sent and summed in bfloat16 or wider, within the bound.
No kernel may reach another device: no remote copies, remote signals or barrier semaphores. Data moves between devices by JAX's collectives and lax.ppermute only.
A program may use at most 64 MiB of HBM per device.

```python
import math
import jax
import jax.numpy as jnp
import numpy as np
from jax import lax

STRETCH = 256
REACH = 2
HEADS = 32
KV = 4
HD = 128
TOKENS = 65536
DOC_MOST = 512
DOCS = 256
N_CP = 128


def aligned_fields(key, lift):
    shape = (2, N_CP, STRETCH, KV, HD)
    base = jax.random.truncated_normal(jax.random.fold_in(key, 5), -4.0, 4.0, shape, jnp.float32)
    signs = 2.0 * jax.random.randint(jax.random.fold_in(key, 6), shape, 0, 2).astype(jnp.float32) - 1.0
    row = jnp.arange(STRETCH)[None, None, :, None, None]
    device = jnp.arange(N_CP)[None, :, None, None, None] + 3 * jnp.arange(2)[:, None, None, None, None]
    level = ((device + row // 8) % 4).astype(jnp.float32)
    chosen = jnp.where((row % 8 == 5) & ((device + row // 8) % 5 == 0), lift, 0.0)
    earlier = jnp.roll(chosen, -1, axis=2)
    strength = 9.0 * (1.0 + level)
    squeeze = jnp.roll(1.0 - 2.0 / (strength * math.sqrt(HD)), -1, axis=2)
    follow = jnp.roll(signs, -1, axis=2)
    key_field = base * (1.0 - chosen - earlier) + chosen * signs + earlier * follow * squeeze
    return (key_field, chosen, strength)


def draw_keys(key, part):
    lift = 0.0
    key_field, chosen, strength = aligned_fields(key, lift)
    return key_field.reshape(2, N_CP, STRETCH, KV * HD).astype(jnp.bfloat16)


def draw_queries(key, part):
    lift = 0.0
    key_field, chosen, strength = aligned_fields(key, lift)
    key = jax.random.fold_in(key, 31)
    shape = (2, N_CP, STRETCH, KV, HEADS // KV, HD)
    base = jax.random.truncated_normal(key, -4.0, 4.0, shape, jnp.float32)
    picked = chosen[..., None]
    aligned = strength[..., None] * key_field[:, :, :, :, None, :]
    field = base * (1.0 - picked) + picked * aligned
    return field.reshape(2, N_CP, STRETCH, HEADS * HD).astype(jnp.bfloat16)


def level_of(stream_key, shape, pieces, low, largest):
    def one(axis_at, blocks):
        steps = jax.random.uniform(jax.random.fold_in(jax.random.fold_in(stream_key, 6), axis_at), (blocks,), jnp.float32, low / len(pieces), largest / len(pieces))
        return jnp.repeat(jnp.exp(steps), shape[axis_at] // blocks).reshape((-1,) + (1,) * (len(shape) - axis_at - 1))

    level = one(*pieces[0])
    for cut in pieces[1:]:
        level = level * one(*cut)
    return level


def length_profile(amount, total, most, skew):
    portions = [(1 << 20) // math.isqrt(grade ** skew) + 1 for grade in range(2, amount + 1)]
    spare, holding = total - most - (amount - 1), [1] * (amount - 1)
    while spare > 0:
        candidates = [i for i in range(amount - 1) if holding[i] < most]
        mass, left = sum([portions[i] for i in candidates]), spare
        for i in candidates:
            addition = min(most - holding[i], max(1, left * portions[i] // mass), spare)
            holding[i] = holding[i] + addition
            spare = spare - addition
    return np.array([most] + holding)


def ragged(own_key, number_of, total, most, skew):
    if number_of == 2:
        one = jax.random.randint(own_key, (), max(1, total - most), min(most, total - 1) + 1)
        return jnp.stack([one, total - one])
    lengths = jnp.asarray(length_profile(number_of, total, most, skew), jnp.int32)
    couples = (number_of - 1) // 2
    giver, taker = lengths[1:1 + 2 * couples:2], lengths[2:2 + 2 * couples:2]
    room = jnp.minimum(giver - 1, most - taker)
    shifted = jax.random.randint(jax.random.fold_in(own_key, 1), (couples,), 0, 1 << 20) % (room + 1)
    lengths = lengths.at[1:1 + 2 * couples:2].set(giver - shifted).at[2:2 + 2 * couples:2].set(taker + shifted)
    return lengths[jax.random.permutation(jax.random.fold_in(own_key, 2), number_of)]


def centred(rng, extent, deviation, bound, cuts=(), kind=jnp.bfloat16):
    factor_of = level_of(rng, extent, cuts, -0.22, 0.18) if cuts else 1.0
    drawn = jax.random.normal(rng, extent, jnp.float32) * deviation * factor_of
    return jnp.minimum(jnp.maximum(drawn, -bound), bound).astype(kind)


def setup_inputs(seed: int = 0) -> dict:
    splits = jax.random.split(jax.random.key(seed), 6)
    queries = draw_queries(jax.random.fold_in(splits[5], 71), 0)
    keys = draw_keys(jax.random.fold_in(splits[5], 71), 0)
    values = centred(splits[2], (2, N_CP, STRETCH, KV * HD), 1.0, 6.0, ((1, 128), (2, 4)))
    out_grad = centred(splits[3], (2, N_CP, STRETCH, HEADS * HD), 1.0, 6.0, ((1, 128), (3, 4)))
    doc_lengths = ragged(splits[4], DOCS, TOKENS, DOC_MOST, 2).astype(jnp.int32)
    return {"queries": queries, "keys": keys, "values": values, "out_grad": out_grad, "doc_lengths": doc_lengths}


def unfold(folded):
    count = folded.shape[1]
    ordered = jnp.concatenate([folded[0], jnp.flip(folded[1], axis=0)], axis=0)
    return ordered.reshape(2 * count * folded.shape[2], folded.shape[3])

def refold(flat, count):
    blocks = flat.reshape(2 * count, -1, flat.shape[-1])
    return jnp.stack([blocks[:count], jnp.flip(blocks[count:], axis=0)])

def reference(queries, keys, values, out_grad, doc_lengths):
    factor = 1.0 / math.sqrt(HD)
    span = REACH * STRETCH
    group_rows = HEADS // KV
    blocks = TOKENS // STRETCH
    query_seq = unfold(queries).reshape(blocks, STRETCH, KV, group_rows, HD)
    grad_seq = unfold(out_grad).reshape(blocks, STRETCH, KV, group_rows, HD)
    key_pad = jnp.concatenate([jnp.zeros((span, KV * HD), keys.dtype), unfold(keys)], axis=0).reshape(-1, KV, HD)
    value_pad = jnp.concatenate([jnp.zeros((span, KV * HD), values.dtype), unfold(values)], axis=0).reshape(-1, KV, HD)
    ends = jnp.cumsum(doc_lengths).astype(jnp.int32)
    positions = jnp.arange(TOKENS, dtype=jnp.int32)
    docs = jnp.searchsorted(ends, positions, side='right').astype(jnp.int32)
    docs_pad = jnp.concatenate([jnp.full((span,), -1, jnp.int32), docs], axis=0)
    best = lax.Precision.HIGHEST

    def one_block(carry, index):
        key_sum, value_sum = carry
        start = (index * STRETCH).astype(jnp.int32)
        key_rows = lax.dynamic_slice_in_dim(key_pad, start, span + STRETCH, 0).astype(jnp.float32)
        value_rows = lax.dynamic_slice_in_dim(value_pad, start, span + STRETCH, 0).astype(jnp.float32)
        key_docs = lax.dynamic_slice_in_dim(docs_pad, start, span + STRETCH, 0)
        query_docs = lax.dynamic_slice_in_dim(docs, start, STRETCH, 0)
        key_pos = start - span + jnp.arange(span + STRETCH, dtype=jnp.int32)
        query_pos = start + jnp.arange(STRETCH, dtype=jnp.int32)
        allowed = (key_docs[None, :] == query_docs[:, None]) & (key_pos[None, :] <= query_pos[:, None])
        allowed = allowed[:, None, None, :]
        query_rows = query_seq[index].astype(jnp.float32)
        grad_rows = grad_seq[index].astype(jnp.float32)
        scores = jnp.einsum('qgrd,kgd->qgrk', query_rows, key_rows, precision=best) * factor
        scores = jnp.where(allowed, scores, -jnp.inf)
        top = lax.optimization_barrier(jnp.max(scores, axis=-1, keepdims=True))
        lse = top + jnp.log(lax.optimization_barrier(jnp.sum(jnp.exp(scores - top), axis=-1, keepdims=True)))
        probs = jnp.exp(scores - lse)
        probs_low = lax.optimization_barrier(probs.astype(jnp.bfloat16)).astype(jnp.float32)
        attn = jnp.einsum('qgrk,kgd->qgrd', probs_low, value_rows, precision=best).astype(jnp.bfloat16)
        delta = lax.optimization_barrier(jnp.sum(attn.astype(jnp.float32) * grad_rows, axis=-1, keepdims=True))
        dprobs = jnp.einsum('qgrd,kgd->qgrk', grad_rows, value_rows, precision=best)
        dscores = lax.optimization_barrier((probs * (dprobs - delta)).astype(jnp.bfloat16)).astype(jnp.float32)
        query_grad = (jnp.einsum('qgrk,kgd->qgrd', dscores, key_rows, precision=best) * factor).astype(jnp.bfloat16)
        key_grad = jnp.einsum('qgrk,qgrd->kgd', dscores, query_rows, precision=best) * factor
        value_grad = jnp.einsum('qgrk,qgrd->kgd', probs_low, grad_rows, precision=best)
        key_sum = lax.dynamic_update_slice_in_dim(key_sum, lax.dynamic_slice_in_dim(key_sum, start, span + STRETCH, 0) + key_grad, start, 0)
        value_sum = lax.dynamic_update_slice_in_dim(value_sum, lax.dynamic_slice_in_dim(value_sum, start, span + STRETCH, 0) + value_grad, start, 0)
        return ((key_sum, value_sum), (attn, query_grad))
    zeros = jnp.zeros((TOKENS + span, KV, HD), jnp.float32)
    (key_sum, value_sum), (attn_all, query_all) = lax.scan(one_block, (zeros, zeros), jnp.arange(blocks, dtype=jnp.int32))
    attn_out = refold(attn_all.reshape(TOKENS, HEADS * HD), N_CP)
    q_grad = refold(query_all.reshape(TOKENS, HEADS * HD), N_CP)
    k_grad = refold(key_sum[span:].reshape(TOKENS, KV * HD).astype(jnp.bfloat16), N_CP)
    v_grad = refold(value_sum[span:].reshape(TOKENS, KV * HD).astype(jnp.bfloat16), N_CP)
    return (attn_out, q_grad, k_grad, v_grad)
```

```python
import functools
import math

import jax
import jax.numpy as jnp
from jax import lax
from jax.experimental import pallas as pl
from jax.experimental.pallas import tpu as pltpu
from jax.sharding import PartitionSpec as P

KV = 4
HD = 128
HEADS_STEP = 2
FACTOR = 1.0 / math.sqrt(HD)
LOG2E = math.log2(math.e)
OUT = -1e30
VMEM = pl.BlockSpec(memory_space=pltpu.VMEM)
FIRST, SECOND = 0, 1


def from_behind(block, axis, distance):
    devices = range(lax.axis_size(axis))
    route = [(i - distance, i) for i in devices if i - distance in devices]
    return lax.ppermute(block, axis, route)


def around(block, axis, distance):
    count = lax.axis_size(axis)
    return lax.ppermute(block, axis, [(i, (i + distance) % count) for i in range(count)])


def dot(a, b, contract):
    return lax.dot_general(a, b, (contract, ((), ())), preferred_element_type=jnp.float32)


def split_kernel(groups, k_ref, v_ref, *pieces):
    tp = lax.axis_index("tp")
    for step, piece in enumerate(pieces, 1):
        lanes = pl.ds(pl.multiple_of(lax.rem(tp + step, groups) * HD, HD), HD)
        piece[:, 0] = k_ref[:, 0, :, lanes]
        piece[:, 1] = v_ref[:, 0, :, lanes]


def join_kernel(groups, k_ref, v_ref, *refs):
    pieces, (both_ref, first_ref, second_ref) = refs[:-3], refs[-3:]
    tp = lax.axis_index("tp")
    rows = k_ref.shape[2]
    lanes = pl.ds(pl.multiple_of(tp * HD, HD), HD)
    place = pl.ds(pl.multiple_of(tp * rows, rows), rows)
    for kind, ref in enumerate((k_ref, v_ref)):
        for half, out in enumerate((first_ref, second_ref)):
            own = ref[half, 0, :, lanes]
            both_ref[half, kind, place, :] = own
            out[kind, place, :] = own
    for step, piece in enumerate(pieces, 1):
        place = pl.ds(pl.multiple_of(lax.rem(tp - step + groups, groups) * rows, rows), rows)
        both_ref[:, :, place, :] = piece[...]
        first_ref[:, place, :] = piece[FIRST]
        second_ref[:, place, :] = piece[SECOND]


def total_kernel(groups, own_ref, up1_ref, up2_ref, down1_ref, down2_ref, *pieces):
    tp = lax.axis_index("tp")
    rows = pieces[0].shape[2]
    for step, piece in enumerate(pieces):
        place = pl.ds(pl.multiple_of(lax.rem(tp + step, groups) * rows, rows), rows)
        for kind in range(2):
            first = (
                own_ref[FIRST, kind, place, :]
                + up1_ref[kind, place, :].astype(jnp.float32)
                + up2_ref[kind, place, :].astype(jnp.float32)
                + down1_ref[1, kind, place, :].astype(jnp.float32)
            )
            second = (
                own_ref[SECOND, kind, place, :]
                + down1_ref[0, kind, place, :].astype(jnp.float32)
                + down2_ref[kind, place, :].astype(jnp.float32)
            )
            piece[FIRST, kind] = first.astype(piece.dtype)
            piece[SECOND, kind] = second.astype(piece.dtype)


def place_kernel(groups, *refs):
    pieces, (k_ref, v_ref) = refs[:-2], refs[-2:]
    tp = lax.axis_index("tp")
    for step, piece in enumerate(pieces):
        lanes = pl.ds(pl.multiple_of(lax.rem(tp - step + groups, groups) * HD, HD), HD)
        k_ref[:, 0, :, lanes] = piece[:, 0]
        v_ref[:, 0, :, lanes] = piece[:, 1]


def blend(field, side):
    low = side // 2
    row = lax.broadcasted_iota(jnp.int32, (low, low), 0)
    column = lax.broadcasted_iota(jnp.int32, (low, low), 1)
    causal = column <= row
    old, own = field[:, :side], field[:, 2 * side :]
    top = jnp.concatenate(
        [jnp.where(causal, own[:low, :low], old[:low, :low]), old[:low, low:]], axis=1
    )
    bottom = jnp.concatenate(
        [own[low:, :low], jnp.where(causal, own[low:, low:], old[low:, low:])], axis=1
    )
    shared = jnp.concatenate([top, bottom], axis=0)
    return jnp.concatenate([shared, field[:, side : 2 * side]], axis=1)


def unblend(field, side):
    low = side // 2
    row = lax.broadcasted_iota(jnp.int32, (low, low), 0)
    column = lax.broadcasted_iota(jnp.int32, (low, low), 1)
    causal = column <= row
    bf = jnp.bfloat16
    none = jnp.zeros((low, low), bf)
    a, d = field[:low, :low], field[low:, low : 2 * low]
    b, c = field[:low, low : 2 * low].astype(bf), field[low:, :low].astype(bf)
    a_own, a_old = jnp.where(causal, a, 0.0).astype(bf), jnp.where(causal, 0.0, a).astype(bf)
    d_own, d_old = jnp.where(causal, d, 0.0).astype(bf), jnp.where(causal, 0.0, d).astype(bf)
    old = jnp.concatenate(
        [jnp.concatenate([a_old, b], axis=1), jnp.concatenate([none, d_old], axis=1)], axis=0
    )
    own = jnp.concatenate(
        [jnp.concatenate([a_own, none], axis=1), jnp.concatenate([c, d_own], axis=1)], axis=0
    )
    return jnp.concatenate([old, field[:, side:].astype(bf), own], axis=1)


def attend_kernel(
    contexts,
    len_ref,
    q_ref,
    g_ref,
    first_ref,
    second_ref,
    up1_ref,
    up2_ref,
    down1_ref,
    down2_ref,
    attn_ref,
    dq_ref,
    own_ref,
    sup1_ref,
    sup2_ref,
    sdown1_ref,
    sdown2_ref,
    k_ref,
    v_ref,
    bias_ref,
    dk_ref,
    dv_ref,
    fold_ref,
):
    side = q_ref.shape[2]
    cp = lax.axis_index("cp")
    last = contexts - 1
    turn, part = pl.program_id(0), pl.program_id(1)
    half = 1 - turn
    block = jnp.where(half == FIRST, cp, 2 * contexts - 1 - cp)
    bf = jnp.bfloat16

    def keep(oldest, middle, own):
        for kind, ref in enumerate((k_ref, v_ref)):
            ref[0:side, :] = oldest(kind)
            ref[side : 2 * side, :] = middle(kind)
            ref[2 * side :, :] = own(kind)

    @pl.when((part == 0) & (half == FIRST))
    def _():
        keep(lambda n: up2_ref[n], lambda n: up1_ref[n], lambda n: first_ref[n])

    @pl.when((part == 0) & (half == SECOND))
    def _():
        @pl.when(cp < last - 1)
        def _():
            keep(lambda n: down2_ref[n], lambda n: down1_ref[SECOND, n], lambda n: second_ref[n])

        @pl.when(cp == last - 1)
        def _():
            keep(
                lambda n: down1_ref[FIRST, n],
                lambda n: down1_ref[SECOND, n],
                lambda n: second_ref[n],
            )

        @pl.when(cp == last)
        def _():
            keep(lambda n: up1_ref[n], lambda n: first_ref[n], lambda n: second_ref[n])

    @pl.when(part == 0)
    def _():
        docs = len_ref.shape[1]
        lengths = jnp.broadcast_to(len_ref[...], (8, docs))
        before = lax.broadcasted_iota(jnp.int32, (docs, docs), 0)
        after = lax.broadcasted_iota(jnp.int32, (docs, docs), 1)
        upto = (before <= after).astype(jnp.float32).astype(bf)
        coarse = (lengths // 16).astype(jnp.float32).astype(bf)
        fine = (lengths % 16).astype(jnp.float32).astype(bf)
        over = ((1,), (0,))
        ends = (16.0 * dot(coarse, upto, over) + dot(fine, upto, over))[0:1, :]
        row = lax.broadcasted_iota(jnp.int32, (side, docs), 0)
        position = (row + block * side).astype(jnp.float32)
        begins = jnp.max(jnp.where(ends <= position, ends, 0.0), axis=1, keepdims=True)
        begins = begins - (block * side).astype(jnp.float32)
        row = lax.broadcasted_iota(jnp.int32, (side, side), 0)
        column = lax.broadcasted_iota(jnp.int32, (side, side), 1)
        key = column.astype(jnp.float32)
        shared = jnp.where(column <= row, key, key - 2.0 * side)
        bias_ref[:, :side] = jnp.where(shared >= begins, 0.0, OUT)
        bias_ref[:, side:] = jnp.where(key - side >= begins, 0.0, OUT)
        dk_ref[...] = jnp.zeros_like(dk_ref)
        dv_ref[...] = jnp.zeros_like(dv_ref)

    keys, values = k_ref[...], v_ref[...]
    along, across = ((1,), (1,)), ((1,), (0,))
    rows_q, rows_g, probs_all, ds_all = [], [], [], []
    for head in range(HEADS_STEP):
        lanes = slice(head * HD, (head + 1) * HD)
        q, g = q_ref[0, 0, :, lanes], g_ref[0, 0, :, lanes]
        scores = blend(dot(q, keys, along), side) * (FACTOR * LOG2E) + bias_ref[...]
        top = jnp.max(scores, axis=1, keepdims=True)
        raised = jnp.exp2(scores - top)
        probs = raised * (1.0 / jnp.sum(raised, axis=1, keepdims=True))
        probs_low = unblend(probs, side)
        attn = dot(probs_low, values, across).astype(bf)
        attn_ref[0, 0, :, lanes] = attn
        delta = jnp.sum(attn.astype(jnp.float32) * g.astype(jnp.float32), axis=1, keepdims=True)
        ds = unblend(probs * (blend(dot(g, values, along), side) - delta), side)
        dq_ref[0, 0, :, lanes] = (dot(ds, keys, across) * FACTOR).astype(bf)
        rows_q.append(q)
        rows_g.append(g)
        probs_all.append(probs_low)
        ds_all.append(ds)
    down = ((0,), (0,))
    dv_ref[...] += dot(jnp.concatenate(rows_g, 0), jnp.concatenate(probs_all, 0), down)
    dk_ref[...] += dot(jnp.concatenate(rows_q, 0), jnp.concatenate(ds_all, 0), down)

    @pl.when(part == pl.num_programs(1) - 1)
    def _():
        terms = (dk_ref[...].T * FACTOR, dv_ref[...].T)

        @pl.when(half == SECOND)
        def _():
            for kind, term in enumerate(terms):
                oldest, middle = term[:side], term[side : 2 * side]
                own_ref[SECOND, kind] = term[2 * side :]
                sdown1_ref[0, kind] = middle.astype(bf)
                sdown1_ref[1, kind] = jnp.where(cp == last - 1, oldest, 0.0).astype(bf)
                sdown2_ref[kind] = oldest.astype(bf)
                fold_ref[kind] = jnp.where(cp == last, term[: 2 * side], 0.0)

        @pl.when(half == FIRST)
        def _():
            for kind, term in enumerate(terms):
                own_ref[FIRST, kind] = term[2 * side :] + fold_ref[kind, side:, :]
                sup1_ref[kind] = (term[side : 2 * side] + fold_ref[kind, :side, :]).astype(bf)
                sup2_ref[kind] = term[:side].astype(bf)


def local(queries, keys, values, out_grad, doc_lengths):
    side, width = queries.shape[2], queries.shape[3]
    contexts, groups = lax.axis_size("cp"), lax.axis_size("tp")
    rows = keys.shape[2]
    bf = jnp.bfloat16
    shape = jax.ShapeDtypeStruct
    piece = shape((2, 2, rows, HD), bf)
    one = shape((2, side, HD), bf)
    two = shape((2, 2, side, HD), bf)

    sent = pl.pallas_call(
        functools.partial(split_kernel, groups),
        out_shape=[piece] * (groups - 1),
        in_specs=[VMEM] * 2,
        out_specs=[VMEM] * (groups - 1),
        name="split",
    )(keys, values)
    came = [around(block, "tp", step) for step, block in enumerate(sent, 1)]
    both, first, second = pl.pallas_call(
        functools.partial(join_kernel, groups),
        out_shape=[two, one, one],
        in_specs=[VMEM] * (groups + 1),
        out_specs=[VMEM] * 3,
        name="join",
    )(keys, values, *came)
    up1 = from_behind(first, "cp", 1)
    up2 = from_behind(first, "cp", 2)
    down1 = from_behind(both, "cp", -1)
    down2 = from_behind(second, "cp", -2)

    lanes = HEADS_STEP * HD
    wide = pl.BlockSpec((1, 1, side, lanes), lambda turn, part: (1 - turn, 0, 0, part))
    work = 2 * (width // HD) * side * 3 * side
    attn_out, q_grad, own, sup1, sup2, sdown1, sdown2 = pl.pallas_call(
        functools.partial(attend_kernel, contexts),
        grid=(2, width // lanes),
        out_shape=[
            shape(queries.shape, bf),
            shape(queries.shape, bf),
            shape((2, 2, side, HD), jnp.float32),
            one,
            one,
            two,
            one,
        ],
        in_specs=[VMEM, wide, wide] + [VMEM] * 6,
        out_specs=[wide, wide] + [VMEM] * 5,
        scratch_shapes=[
            pltpu.VMEM((3 * side, HD), bf),
            pltpu.VMEM((3 * side, HD), bf),
            pltpu.VMEM((side, 2 * side), jnp.float32),
            pltpu.VMEM((HD, 3 * side), jnp.float32),
            pltpu.VMEM((HD, 3 * side), jnp.float32),
            pltpu.VMEM((2, 2 * side, HD), jnp.float32),
        ],
        compiler_params=pltpu.CompilerParams(vmem_limit_bytes=40 * 2**20),
        cost_estimate=pl.CostEstimate(
            flops=12 * work * HD, bytes_accessed=8 * side * width * 2, transcendentals=work
        ),
        name="attend",
    )(doc_lengths[None, :], queries, out_grad, first, second, up1, up2, down1, down2)

    back_up1 = from_behind(sup1, "cp", -1)
    back_up2 = from_behind(sup2, "cp", -2)
    back_down1 = from_behind(sdown1, "cp", 1)
    back_down2 = from_behind(sdown2, "cp", 2)
    pieces = pl.pallas_call(
        functools.partial(total_kernel, groups),
        out_shape=[piece] * groups,
        in_specs=[VMEM] * 5,
        out_specs=[VMEM] * groups,
        name="total",
    )(own, back_up1, back_up2, back_down1, back_down2)
    returned = [pieces[0]] + [around(block, "tp", step) for step, block in enumerate(pieces[1:], 1)]
    k_grad, v_grad = pl.pallas_call(
        functools.partial(place_kernel, groups),
        out_shape=[shape(keys.shape, bf)] * 2,
        in_specs=[VMEM] * groups,
        out_specs=[VMEM] * 2,
        name="place",
    )(*returned)
    return (attn_out, q_grad, k_grad, v_grad)


def solution(mesh):
    heads, tokens = P(None, "cp", None, "tp"), P(None, "cp", "tp", None)
    return jax.shard_map(
        local,
        mesh=mesh,
        in_specs=(heads, tokens, tokens, heads, P()),
        out_specs=(heads, heads, tokens, tokens),
        check_vma=False,
    )
```

```python
import functools
import math

import jax
import jax.numpy as jnp
from jax import lax
from jax.experimental import pallas as pl
from jax.experimental.pallas import tpu as pltpu
from jax.sharding import PartitionSpec as P

HD = 128
HEADS_STEP = 4
FACTOR = 1.0 / math.sqrt(HD)
LOG2E = math.log2(math.e)
OUT = -1e30
VMEM = pl.BlockSpec(memory_space=pltpu.VMEM)
HBM = pl.BlockSpec(memory_space=pltpu.HBM)
ANY = pl.BlockSpec(memory_space=pl.ANY)
SMALL = pltpu.CompilerParams(vmem_limit_bytes=4 * 2**20)


def device_at(place, contexts):
    return 2 * place if 2 * place < contexts else 2 * (contexts - 1 - place) + 1


def along_line(block, step):
    contexts = lax.axis_size("cp")
    places = range(contexts)
    route = [
        (device_at(i, contexts), device_at(i + step, contexts)) for i in places if i + step in places
    ]
    return lax.ppermute(block, "cp", route)


def to_partner(block):
    return lax.ppermute(block, "cp", [(i, i ^ 1) for i in range(lax.axis_size("cp"))])


def offset(step, core, groups):
    return jnp.where(core == 0, step, groups - step)


def around(block, step):
    contexts, groups = lax.axis_size("cp"), lax.axis_size("tp")
    route = []
    for i in range(contexts):
        turn = step if i % 2 == 0 else groups - step
        route += [(i * groups + t, i * groups + (t + turn) % groups) for t in range(groups)]
    return lax.ppermute(block, ("cp", "tp"), route)


def dot(a, b, contract):
    return lax.dot_general(a, b, (contract, ((), ())), preferred_element_type=jnp.float32)


def aligned(index, size):
    return pl.ds(pl.multiple_of(index * size, size), size)


def split_kernel(groups, k_ref, v_ref, k_pair_ref, v_pair_ref, *pieces):
    tp, core = lax.axis_index("tp"), lax.rem(lax.axis_index("cp"), 2)
    for step, piece in enumerate(pieces, 1):
        lanes = aligned(lax.rem(tp + offset(step, core, groups), groups), HD)
        for block, refs in enumerate(((k_ref, v_ref), (k_pair_ref, v_pair_ref))):
            for kind, ref in enumerate(refs):
                piece[block, kind] = ref[core, 0, :, lanes]


def join_kernel(groups, k_ref, v_ref, k_pair_ref, v_pair_ref, *refs):
    pieces, out_ref = refs[:-1], refs[-1]
    tp, core = lax.axis_index("tp"), lax.rem(lax.axis_index("cp"), 2)
    rows = k_ref.shape[2]
    for block, pair in enumerate(((k_ref, v_ref), (k_pair_ref, v_pair_ref))):
        for kind, ref in enumerate(pair):
            out_ref[kind, aligned(block * groups + tp, rows), :] = ref[core, 0, :, aligned(tp, HD)]
    for step, piece in enumerate(pieces, 1):
        source = lax.rem(tp - offset(step, core, groups) + groups, groups)
        for block in range(2):
            out_ref[:, aligned(block * groups + source, rows), :] = piece[block]


def total_kernel(groups, own_ref, came_ref, *pieces):
    tp, core = lax.axis_index("tp"), lax.rem(lax.axis_index("cp"), 2)
    rows = pieces[0].shape[2]
    for step, piece in enumerate(pieces):
        target = lax.rem(tp + offset(step, core, groups), groups)
        for block in range(2):
            place = aligned(block * groups + target, rows)
            total = own_ref[:, place, :] + came_ref[:, place, :].astype(jnp.float32)
            piece[block] = total.astype(piece.dtype)


def place_kernel(groups, *refs):
    pieces, outs = refs[:-3], refs[-2:]
    tp, core = lax.axis_index("tp"), lax.rem(lax.axis_index("cp"), 2)
    for step, piece in enumerate(pieces):
        lanes = aligned(lax.rem(tp - offset(step, core, groups) + groups, groups), HD)
        for block, out in enumerate(outs):
            out[:, :, lanes] = piece[block]


def finish_kernel(kept_ref, came_ref, k_ref, v_ref):
    core = lax.rem(lax.axis_index("cp"), 2)
    for kind, ref in enumerate((k_ref, v_ref)):
        ref[core, 0] = kept_ref[kind]
        ref[1 - core, 0] = came_ref[kind]


def pick_kernel(q_ref, g_ref, after_ref, own_ref, pair_ref, sems):
    core = lax.rem(lax.axis_index("cp"), 2)
    copies = []
    for kind, ref in enumerate((q_ref, g_ref)):
        copies.append(pltpu.make_async_copy(ref.at[1 - core, 0], pair_ref.at[kind], sems.at[kind]))
        copies.append(pltpu.make_async_copy(ref.at[core, 0], own_ref.at[kind], sems.at[2 + kind]))
    for copy in copies:
        copy.start()
    for copy in copies:
        copy.wait()


def fill_kernel(attn_in, dq_in, came_ref, after_ref, attn_ref, dq_ref, done_ref, sems):
    core = lax.rem(lax.axis_index("cp"), 2)
    copies = [
        pltpu.make_async_copy(came_ref.at[kind], ref.at[1 - core, 0], sems.at[kind])
        for kind, ref in enumerate((attn_ref, dq_ref))
    ]
    for copy in copies:
        copy.start()
    done_ref[...] = jnp.zeros_like(done_ref)
    for copy in copies:
        copy.wait()


def blend(field, side):
    low = side // 2
    row = lax.broadcasted_iota(jnp.int32, (low, low), 0)
    column = lax.broadcasted_iota(jnp.int32, (low, low), 1)
    causal = column <= row
    old, own = field[:, :side], field[:, 2 * side :]
    top = jnp.concatenate(
        [jnp.where(causal, own[:low, :low], old[:low, :low]), old[:low, low:]], axis=1
    )
    bottom = jnp.concatenate(
        [own[low:, :low], jnp.where(causal, own[low:, low:], old[low:, low:])], axis=1
    )
    shared = jnp.concatenate([top, bottom], axis=0)
    return jnp.concatenate([shared, field[:, side : 2 * side]], axis=1)


def unblend(field, side):
    low = side // 2
    row = lax.broadcasted_iota(jnp.int32, (low, low), 0)
    column = lax.broadcasted_iota(jnp.int32, (low, low), 1)
    causal = column <= row
    bf = jnp.bfloat16
    none = jnp.zeros((low, low), bf)
    a, d = field[:low, :low], field[low:, low : 2 * low]
    b, c = field[:low, low : 2 * low].astype(bf), field[low:, :low].astype(bf)
    a_own, a_old = jnp.where(causal, a, 0.0).astype(bf), jnp.where(causal, 0.0, a).astype(bf)
    d_own, d_old = jnp.where(causal, d, 0.0).astype(bf), jnp.where(causal, 0.0, d).astype(bf)
    old = jnp.concatenate(
        [jnp.concatenate([a_old, b], axis=1), jnp.concatenate([none, d_old], axis=1)], axis=0
    )
    own = jnp.concatenate(
        [jnp.concatenate([a_own, none], axis=1), jnp.concatenate([c, d_own], axis=1)], axis=0
    )
    return jnp.concatenate([old, field[:, side:].astype(bf), own], axis=1)


def attend_kernel(
    where_ref,
    len_ref,
    own_qg_ref,
    pair_qg_ref,
    behind_ref,
    here_ref,
    attn_ref,
    dq_ref,
    pair_ref,
    own_ref,
    halo_ref,
    k_ref,
    v_ref,
    kt_ref,
    vt_ref,
    bias_ref,
    dk_ref,
    dv_ref,
):
    side = own_qg_ref.shape[1]
    turn, part = pl.program_id(0), pl.program_id(1)
    bf = jnp.bfloat16

    @pl.when((turn == 0) & (part == 0))
    def _():
        for kind, (ref, turned) in enumerate(((k_ref, kt_ref), (v_ref, vt_ref))):
            ref[: 2 * side, :] = behind_ref[kind]
            ref[2 * side :, :] = here_ref[kind]
            turned[:, : 2 * side] = behind_ref[kind].T
            turned[:, 2 * side :] = here_ref[kind].T
        dk_ref[...] = jnp.zeros_like(dk_ref)
        dv_ref[...] = jnp.zeros_like(dv_ref)

    @pl.when(part == 0)
    def _():
        begin_block = (2 * where_ref[1] + turn) * side
        docs = len_ref.shape[1]
        lengths = jnp.broadcast_to(len_ref[...], (8, docs))
        before = lax.broadcasted_iota(jnp.int32, (docs, docs), 0)
        after = lax.broadcasted_iota(jnp.int32, (docs, docs), 1)
        upto = (before <= after).astype(jnp.float32).astype(bf)
        coarse = (lengths // 16).astype(jnp.float32).astype(bf)
        fine = (lengths % 16).astype(jnp.float32).astype(bf)
        over = ((1,), (0,))
        ends = (16.0 * dot(coarse, upto, over) + dot(fine, upto, over))[0:1, :]
        row = lax.broadcasted_iota(jnp.int32, (side, docs), 0)
        position = (row + begin_block).astype(jnp.float32)
        begins = jnp.max(jnp.where(ends <= position, ends, 0.0), axis=1, keepdims=True)
        begins = begins - begin_block.astype(jnp.float32)
        row = lax.broadcasted_iota(jnp.int32, (side, side), 0)
        column = lax.broadcasted_iota(jnp.int32, (side, side), 1)
        key = column.astype(jnp.float32)
        shared = jnp.where(column <= row, key, key - 2.0 * side)
        bias_ref[:, :side] = jnp.where(shared >= begins, 0.0, OUT)
        bias_ref[:, side:] = jnp.where(key - side >= begins, 0.0, OUT)

    window = pl.ds(pl.multiple_of(turn * side, side), 3 * side)
    over, down = ((1,), (0,)), ((0,), (0,))

    def run(take_q, take_g, give):
        def products(head):
            q, g = take_q(head), take_g(head)
            scores = dot(q, kt_ref[:, window], over)
            return q, g, scores, dot(g, vt_ref[:, window], over)

        def softmax(scores):
            scaled = blend(scores, side) * (FACTOR * LOG2E) + bias_ref[...]
            raised = jnp.exp2(scaled - jnp.max(scaled, axis=1, keepdims=True))
            return raised * (1.0 / jnp.sum(raised, axis=1, keepdims=True))

        def finish(head, q, g, probs_low, ds):
            give(1, head, (dot(ds, k_ref[window, :], over) * FACTOR).astype(bf))
            dv_ref[:, window] += dot(g, probs_low, down)
            dk_ref[:, window] += dot(q, ds, down)

        pending = None
        ahead = products(0)
        for head in range(HEADS_STEP):
            q, g, scores, dprobs = ahead
            if head + 1 < HEADS_STEP:
                ahead = products(head + 1)
            probs = softmax(scores)
            probs_low = unblend(probs, side)
            attn = dot(probs_low, v_ref[window, :], over).astype(bf)
            give(0, head, attn)
            if pending is not None:
                finish(*pending)
            delta = jnp.sum(
                attn.astype(jnp.float32) * g.astype(jnp.float32), axis=1, keepdims=True
            )
            ds = unblend(probs * (blend(dprobs, side) - delta), side)
            pending = (head, q, g, probs_low, ds)
        finish(*pending)

    def lanes(head):
        return slice(head * HD, (head + 1) * HD)

    def taker(ref, kind):
        return lambda head: ref[kind, :, aligned(part * HEADS_STEP + head, HD)]

    @pl.when(turn == 0)
    def _():
        outs = (attn_ref, dq_ref)

        def give(kind, head, value):
            outs[kind][0, 0, :, lanes(head)] = value

        run(taker(own_qg_ref, 0), taker(own_qg_ref, 1), give)

    @pl.when(turn == 1)
    def _():
        def give(kind, head, value):
            pair_ref[kind, :, lanes(head)] = value

        run(taker(pair_qg_ref, 0), taker(pair_qg_ref, 1), give)

    @pl.when((turn == 1) & (part == pl.num_programs(1) - 1))
    def _():
        for kind, (ref, factor) in enumerate(((dk_ref, FACTOR), (dv_ref, 1.0))):
            halo_ref[kind] = (ref[:, : 2 * side].T * factor).astype(bf)
            own_ref[kind] = ref[:, 2 * side :].T * factor


def local(queries, keys, values, out_grad, doc_lengths):
    side, width = queries.shape[2], queries.shape[3]
    contexts, groups = lax.axis_size("cp"), lax.axis_size("tp")
    rows = keys.shape[2]
    bf = jnp.bfloat16
    shape = jax.ShapeDtypeStruct
    piece = shape((2, 2, rows, HD), bf)
    cp = lax.axis_index("cp")
    core = cp % 2
    place = jnp.where(core == 0, cp // 2, contexts - 1 - cp // 2)

    local_kv = (keys, values, to_partner(keys), to_partner(values))
    sent = pl.pallas_call(
        functools.partial(split_kernel, groups),
        out_shape=[piece] * (groups - 1),
        in_specs=[VMEM] * 4,
        out_specs=[VMEM] * (groups - 1),
        compiler_params=SMALL,
        name="split",
    )(*local_kv)
    came = [around(block, step) for step, block in enumerate(sent, 1)]
    both = shape((2, side, width), bf)
    own_qg, for_pair = pl.pallas_call(
        pick_kernel,
        out_shape=[both] * 2,
        in_specs=[HBM, HBM, ANY],
        out_specs=[VMEM] * 2,
        scratch_shapes=[pltpu.SemaphoreType.DMA((4,))],
        compiler_params=SMALL,
        name="pick",
    )(queries, out_grad, came[0])
    pair_qg = to_partner(for_pair)
    here = pl.pallas_call(
        functools.partial(join_kernel, groups),
        out_shape=shape((2, 2 * side, HD), bf),
        in_specs=[VMEM] * (groups + 3),
        out_specs=VMEM,
        compiler_params=SMALL,
        name="join",
    )(*local_kv, *came)
    behind = along_line(here, 1)

    lanes = HEADS_STEP * HD
    parts = width // lanes
    own_turn = pl.BlockSpec(
        (1, 1, side, lanes), lambda j, n, at: (at[0], 0, 0, jnp.where(j == 0, n, parts - 1))
    )
    pair_out = pl.BlockSpec((2, side, lanes), lambda j, n, at: (0, 0, jnp.where(j == 0, 0, n)))
    work = 2 * (width // HD) * side * 3 * side
    attn_out, q_grad, for_pair, own, halo = pl.pallas_call(
        attend_kernel,
        grid_spec=pltpu.PrefetchScalarGridSpec(
            num_scalar_prefetch=1,
            grid=(2, parts),
            in_specs=[VMEM] * 5,
            out_specs=[own_turn, own_turn, pair_out, VMEM, VMEM],
            scratch_shapes=[
                pltpu.VMEM((4 * side, HD), bf),
                pltpu.VMEM((4 * side, HD), bf),
                pltpu.VMEM((HD, 4 * side), bf),
                pltpu.VMEM((HD, 4 * side), bf),
                pltpu.VMEM((side, 2 * side), jnp.float32),
                pltpu.VMEM((HD, 4 * side), jnp.float32),
                pltpu.VMEM((HD, 4 * side), jnp.float32),
            ],
        ),
        out_shape=[
            shape(queries.shape, bf),
            shape(queries.shape, bf),
            both,
            shape((2, 2 * side, HD), jnp.float32),
            shape((2, 2 * side, HD), bf),
        ],
        compiler_params=pltpu.CompilerParams(vmem_limit_bytes=32 * 2**20),
        cost_estimate=pl.CostEstimate(
            flops=12 * work * HD, bytes_accessed=8 * side * width * 2, transcendentals=work
        ),
        name="attend",
    )(
        jnp.stack([core, place]),
        doc_lengths[None, :],
        own_qg,
        pair_qg,
        behind,
        here,
    )

    came_halo = along_line(halo, -1)
    from_pair = to_partner(for_pair)
    pieces = pl.pallas_call(
        functools.partial(total_kernel, groups),
        out_shape=[piece] * groups,
        in_specs=[VMEM] * 2,
        out_specs=[VMEM] * groups,
        compiler_params=SMALL,
        name="total",
    )(own, came_halo)
    returned = [pieces[0]] + [around(block, step) for step, block in enumerate(pieces[1:], 1)]
    attn_out, q_grad, filled = pl.pallas_call(
        fill_kernel,
        out_shape=[shape(queries.shape, bf)] * 2 + [shape((8, HD), jnp.float32)],
        in_specs=[HBM, HBM, ANY, ANY],
        out_specs=[HBM, HBM, VMEM],
        scratch_shapes=[pltpu.SemaphoreType.DMA((2,))],
        input_output_aliases={0: 0, 1: 1},
        compiler_params=SMALL,
        name="fill",
    )(attn_out, q_grad, from_pair, returned[1])
    kept, for_pair = pl.pallas_call(
        functools.partial(place_kernel, groups),
        out_shape=[shape((2, rows, keys.shape[3]), bf)] * 2,
        in_specs=[VMEM] * groups + [ANY],
        out_specs=[VMEM] * 2,
        compiler_params=SMALL,
        name="place",
    )(*returned, filled)
    k_grad, v_grad = pl.pallas_call(
        finish_kernel,
        out_shape=[shape(keys.shape, bf)] * 2,
        in_specs=[VMEM] * 2,
        out_specs=[VMEM] * 2,
        compiler_params=SMALL,
        name="finish",
    )(kept, to_partner(for_pair))

    return (attn_out, q_grad, k_grad, v_grad)


def solution(mesh):
    heads, tokens = P(None, "cp", None, "tp"), P(None, "cp", "tp", None)
    return jax.shard_map(
        local,
        mesh=mesh,
        in_specs=(heads, tokens, tokens, heads, P()),
        out_specs=(heads, heads, tokens, tokens),
        check_vma=False,
    )
```

```python
import functools
import math

import jax
import jax.numpy as jnp
from jax import lax
from jax.experimental import pallas as pl
from jax.experimental.pallas import tpu as pltpu
from jax.sharding import PartitionSpec as P

HD = 128
FACTOR = 1.0 / math.sqrt(HD)
LOG2E = math.log2(math.e)
OUT = -1e30
VMEM = pl.BlockSpec(memory_space=pltpu.VMEM)
HBM = pl.BlockSpec(memory_space=pltpu.HBM)
ANY = pl.BlockSpec(memory_space=pl.ANY)
SMALL = pltpu.CompilerParams(vmem_limit_bytes=4 * 2**20)


def device_at(place, contexts):
    return 2 * place if 2 * place < contexts else 2 * (contexts - 1 - place) + 1


def along_line(block, step):
    contexts = lax.axis_size("cp")
    places = range(contexts)
    route = [
        (device_at(i, contexts), device_at(i + step, contexts)) for i in places if i + step in places
    ]
    return lax.ppermute(block, "cp", route)


def to_partner(block):
    return lax.ppermute(block, "cp", [(i, i ^ 1) for i in range(lax.axis_size("cp"))])


def offset(step, core, groups):
    return jnp.where(core == 0, step, groups - step)


def around(block, step):
    contexts, groups = lax.axis_size("cp"), lax.axis_size("tp")
    route = []
    for i in range(contexts):
        turn = step if i % 2 == 0 else groups - step
        route += [(i * groups + t, i * groups + (t + turn) % groups) for t in range(groups)]
    return lax.ppermute(block, ("cp", "tp"), route)


def dot(a, b, contract):
    return lax.dot_general(a, b, (contract, ((), ())), preferred_element_type=jnp.float32)


def aligned(index, size):
    return pl.ds(pl.multiple_of(index * size, size), size)


def split_kernel(groups, kv_ref, kv_pair_ref, *pieces):
    tp, core = lax.axis_index("tp"), lax.rem(lax.axis_index("cp"), 2)
    for step, piece in enumerate(pieces, 1):
        lanes = aligned(lax.rem(tp + offset(step, core, groups), groups), HD)
        for block, ref in enumerate((kv_ref, kv_pair_ref)):
            for kind in range(2):
                piece[block, kind] = ref[kind, core, 0, :, lanes]


def join_kernel(groups, kv_ref, kv_pair_ref, *refs):
    pieces, out_ref = refs[:-2], refs[-1]
    tp, core = lax.axis_index("tp"), lax.rem(lax.axis_index("cp"), 2)
    rows = kv_ref.shape[3]
    for block, ref in enumerate((kv_ref, kv_pair_ref)):
        place = aligned(block * groups + tp, rows)
        for kind in range(2):
            out_ref[kind, place, :] = ref[kind, core, 0, :, aligned(tp, HD)]
    for step, piece in enumerate(pieces, 1):
        source = lax.rem(tp - offset(step, core, groups) + groups, groups)
        for block in range(2):
            out_ref[:, aligned(block * groups + source, rows), :] = piece[block]


def total_kernel(groups, own_ref, came_ref, *pieces):
    tp, core = lax.axis_index("tp"), lax.rem(lax.axis_index("cp"), 2)
    rows = pieces[0].shape[2]
    for step, piece in enumerate(pieces):
        target = lax.rem(tp + offset(step, core, groups), groups)
        for block in range(2):
            place = aligned(block * groups + target, rows)
            total = own_ref[:, place, :] + came_ref[:, place, :].astype(jnp.float32)
            piece[block] = total.astype(piece.dtype)


def place_kernel(groups, *refs):
    pieces, outs = refs[:-3], refs[-2:]
    tp, core = lax.axis_index("tp"), lax.rem(lax.axis_index("cp"), 2)
    for step, piece in enumerate(pieces):
        lanes = aligned(lax.rem(tp - offset(step, core, groups) + groups, groups), HD)
        for block, out in enumerate(outs):
            out[:, :, lanes] = piece[block]


def finish_kernel(kept_ref, came_ref, k_ref, v_ref):
    core = lax.rem(lax.axis_index("cp"), 2)
    for kind, ref in enumerate((k_ref, v_ref)):
        ref[core, 0] = kept_ref[kind]
        ref[1 - core, 0] = came_ref[kind]


def prepare_kernel(contexts, q_ref, g_ref, len_ref, qg_ref, bias_ref, sems):
    chip, core = lax.axis_index("cp") // 2, lax.rem(lax.axis_index("cp"), 2)
    copies = []
    for kind, ref in enumerate((q_ref, g_ref)):
        for turn, half in enumerate((1 - core, core)):
            copies.append(
                pltpu.make_async_copy(
                    ref.at[half, 0], qg_ref.at[kind, turn], sems.at[2 * kind + turn]
                )
            )
    for copy in copies:
        copy.start()

    bf = jnp.bfloat16
    side, docs = bias_ref.shape[1], len_ref.shape[1]
    up, back = chip, contexts - 1 - chip
    blocks = (2 * jnp.where(core == 0, back, up) + 1, 2 * jnp.where(core == 0, up, back))
    lengths = jnp.broadcast_to(len_ref[...], (8, docs))
    before = lax.broadcasted_iota(jnp.int32, (docs, docs), 0)
    after = lax.broadcasted_iota(jnp.int32, (docs, docs), 1)
    upto = (before <= after).astype(jnp.float32).astype(bf)
    coarse = (lengths // 16).astype(jnp.float32).astype(bf)
    fine = (lengths % 16).astype(jnp.float32).astype(bf)
    over = ((1,), (0,))
    ends = (16.0 * dot(coarse, upto, over) + dot(fine, upto, over))[0:1, :]
    row = lax.broadcasted_iota(jnp.int32, (side, side), 0)
    column = lax.broadcasted_iota(jnp.int32, (side, side), 1)
    key = column.astype(jnp.float32)
    shared = jnp.where(column <= row, key, key - 2.0 * side)
    for turn, block in enumerate(blocks):
        first = block * side
        position = lax.broadcasted_iota(jnp.int32, (side, docs), 0) + first
        begins = jnp.where(ends <= position.astype(jnp.float32), ends, 0.0)
        begins = jnp.max(begins, axis=1, keepdims=True) - first.astype(jnp.float32)
        bias_ref[turn, :, :side] = jnp.where(shared >= begins, 0.0, OUT)
        bias_ref[turn, :, side:] = jnp.where(key - side >= begins, 0.0, OUT)

    for copy in copies:
        copy.wait()


def merge_kernel(mine_ref, came_ref, halo_ref, own_ref):
    side = mine_ref.shape[1] // 3
    for kind in range(2):
        mine = [mine_ref[kind, n * side : (n + 1) * side, :] for n in range(3)]
        came = [
            came_ref[kind, n * side : (n + 1) * side, :].astype(jnp.float32) for n in range(3)
        ]
        halo_ref[kind, :side, :] = mine[0].astype(halo_ref.dtype)
        halo_ref[kind, side:, :] = (mine[1] + came[0]).astype(halo_ref.dtype)
        own_ref[kind, :side, :] = mine[2] + came[1]
        own_ref[kind, side:, :] = came[2]


def fill_kernel(*refs):
    parts, (after_ref, attn_ref, dq_ref, done_ref, sems) = refs[:4], refs[4:]
    core = lax.rem(lax.axis_index("cp"), 2)
    copies = []
    for kind, ref in enumerate((attn_ref, dq_ref)):
        for turn, half in enumerate((1 - core, core)):
            n = 2 * kind + turn
            copies.append(pltpu.make_async_copy(parts[n], ref.at[half, 0], sems.at[n]))
    for copy in copies:
        copy.start()
    done_ref[...] = jnp.zeros_like(done_ref)
    for copy in copies:
        copy.wait()


def blend(field, side):
    low = side // 2
    row = lax.broadcasted_iota(jnp.int32, (low, low), 0)
    column = lax.broadcasted_iota(jnp.int32, (low, low), 1)
    causal = column <= row
    old, own = field[:, :side], field[:, 2 * side :]
    top = jnp.concatenate(
        [jnp.where(causal, own[:low, :low], old[:low, :low]), old[:low, low:]], axis=1
    )
    bottom = jnp.concatenate(
        [own[low:, :low], jnp.where(causal, own[low:, low:], old[low:, low:])], axis=1
    )
    shared = jnp.concatenate([top, bottom], axis=0)
    return jnp.concatenate([shared, field[:, side : 2 * side]], axis=1)


def unblend(field, side):
    low = side // 2
    row = lax.broadcasted_iota(jnp.int32, (low, low), 0)
    column = lax.broadcasted_iota(jnp.int32, (low, low), 1)
    causal = column <= row
    bf = jnp.bfloat16
    none = jnp.zeros((low, low), bf)
    a, d = field[:low, :low], field[low:, low : 2 * low]
    b, c = field[:low, low : 2 * low].astype(bf), field[low:, :low].astype(bf)
    a_own, a_old = jnp.where(causal, a, 0.0).astype(bf), jnp.where(causal, 0.0, a).astype(bf)
    d_own, d_old = jnp.where(causal, d, 0.0).astype(bf), jnp.where(causal, 0.0, d).astype(bf)
    old = jnp.concatenate(
        [jnp.concatenate([a_old, b], axis=1), jnp.concatenate([none, d_old], axis=1)], axis=0
    )
    own = jnp.concatenate(
        [jnp.concatenate([a_own, none], axis=1), jnp.concatenate([c, d_own], axis=1)], axis=0
    )
    return jnp.concatenate([old, field[:, side:].astype(bf), own], axis=1)


def line_window(behind_ref, here_ref, kind, turn, side):
    if turn == 0:
        parts = (behind_ref[kind, side:, :], here_ref[kind])
    else:
        parts = (behind_ref[kind], here_ref[kind, :side, :])
    return jnp.concatenate(parts, axis=0)


def attend_kernel(
    turn, qg_ref, behind_ref, here_ref, bias_ref, attn_ref, ds_ref, grad_ref, kt_ref, vt_ref, dk_ref, dv_ref
):
    side, heads = attn_ref.shape[0], ds_ref.shape[0]
    bf = jnp.bfloat16
    over, down = ((1,), (0,)), ((0,), (0,))
    values = line_window(behind_ref, here_ref, 1, turn, side)
    kt_ref[...] = line_window(behind_ref, here_ref, 0, turn, side).T
    vt_ref[...] = values.T

    def lanes(head):
        return slice(head * HD, (head + 1) * HD)

    def products(head):
        q, g = qg_ref[0, turn, :, lanes(head)], qg_ref[1, turn, :, lanes(head)]
        return q, g, dot(q, kt_ref[...], over), dot(g, vt_ref[...], over)

    def softmax(scores):
        scaled = blend(scores, side) * (FACTOR * LOG2E) + bias_ref[turn]
        raised = jnp.exp2(scaled - jnp.max(scaled, axis=1, keepdims=True))
        return raised * (1.0 / jnp.sum(raised, axis=1, keepdims=True))

    def finish(head, q, g, probs_low, ds):
        ds_ref[head] = ds
        value_term, key_term = dot(g, probs_low, down), dot(q, ds, down)
        if head == 0:
            dv_ref[...], dk_ref[...] = value_term, key_term
        else:
            dv_ref[...] += value_term
            dk_ref[...] += key_term

    pending = None
    ahead = products(0)
    for head in range(heads):
        q, g, scores, dprobs = ahead
        if head + 1 < heads:
            ahead = products(head + 1)
        probs = softmax(scores)
        probs_low = unblend(probs, side)
        attn = dot(probs_low, values, over).astype(bf)
        attn_ref[:, lanes(head)] = attn
        if pending is not None:
            finish(*pending)
        delta = jnp.sum(attn.astype(jnp.float32) * g.astype(jnp.float32), axis=1, keepdims=True)
        ds = unblend(probs * (blend(dprobs, side) - delta), side)
        pending = (head, q, g, probs_low, ds)
    finish(*pending)
    grad_ref[0] = (dk_ref[...].T * FACTOR).astype(grad_ref.dtype)
    grad_ref[1] = dv_ref[...].T.astype(grad_ref.dtype)


def query_kernel(*refs):
    inputs, outs = refs[:-2], refs[-2:]
    for turn, out in enumerate(outs):
        ds_ref, behind_ref, here_ref = inputs[3 * turn : 3 * turn + 3]
        heads, side = ds_ref.shape[0], ds_ref.shape[1]
        keys = line_window(behind_ref, here_ref, 0, turn, side)
        for head in range(heads):
            dq = dot(ds_ref[head], keys, ((1,), (0,))) * FACTOR
            out[:, head * HD : (head + 1) * HD] = dq.astype(out.dtype)


def local(queries, keys, values, out_grad, doc_lengths):
    side, width = queries.shape[2], queries.shape[3]
    contexts, groups = lax.axis_size("cp"), lax.axis_size("tp")
    rows = keys.shape[2]
    bf = jnp.bfloat16
    shape = jax.ShapeDtypeStruct
    piece = shape((2, 2, rows, HD), bf)

    kv = jnp.stack([keys, values])
    local_kv = (kv, to_partner(kv))
    sent = pl.pallas_call(
        functools.partial(split_kernel, groups),
        out_shape=[piece] * (groups - 1),
        in_specs=[VMEM] * 2,
        out_specs=[VMEM] * (groups - 1),
        compiler_params=SMALL,
        name="split",
    )(*local_kv)
    came = [around(block, step) for step, block in enumerate(sent, 1)]
    qg, bias = pl.pallas_call(
        functools.partial(prepare_kernel, contexts),
        out_shape=[shape((2, 2, side, width), bf), shape((2, side, 2 * side), jnp.float32)],
        in_specs=[HBM, HBM, VMEM],
        out_specs=[VMEM] * 2,
        scratch_shapes=[pltpu.SemaphoreType.DMA((4,))],
        compiler_params=SMALL,
        cost_estimate=pl.CostEstimate(
            flops=0, bytes_accessed=16 * side * width, transcendentals=0
        ),
        name="prepare",
    )(queries, out_grad, doc_lengths[None, :])
    here = pl.pallas_call(
        functools.partial(join_kernel, groups),
        out_shape=shape((2, 2 * side, HD), bf),
        in_specs=[VMEM] * (groups + 1) + [ANY],
        out_specs=VMEM,
        compiler_params=SMALL,
        name="join",
    )(*local_kv, *came, bias)
    behind = along_line(here, 1)
    here_pair, behind_pair = to_partner(here), to_partner(behind)
    heads = width // HD
    work = heads * side * 3 * side
    half = shape((side, width), bf)
    reach = (2, 3 * side, HD)

    def attend(turn, grad_type, *line):
        return pl.pallas_call(
            functools.partial(attend_kernel, turn),
            in_specs=[VMEM] * 4,
            out_specs=[VMEM] * 3,
            scratch_shapes=[pltpu.VMEM((HD, 3 * side), bf)] * 2
            + [pltpu.VMEM((HD, 3 * side), jnp.float32)] * 2,
            out_shape=[half, shape((heads, side, 3 * side), bf), shape(reach, grad_type)],
            compiler_params=pltpu.CompilerParams(vmem_limit_bytes=32 * 2**20),
            cost_estimate=pl.CostEstimate(
                flops=10 * work * HD, bytes_accessed=6 * side * width, transcendentals=work
            ),
            name="attend",
        )(qg, *line, bias)

    attn_pair, ds_pair, grad_pair = attend(0, bf, behind_pair, here_pair)
    came_grad = to_partner(grad_pair)
    attn_own, ds_own, grad_own = attend(1, jnp.float32, behind, here)
    halo, own = pl.pallas_call(
        merge_kernel,
        out_shape=[shape((2, 2 * side, HD), bf), shape((2, 2 * side, HD), jnp.float32)],
        in_specs=[VMEM] * 2,
        out_specs=[VMEM] * 2,
        compiler_params=SMALL,
        name="merge",
    )(grad_own, came_grad)
    came_halo = along_line(halo, -1)
    dq_pair, dq_own = pl.pallas_call(
        query_kernel,
        out_shape=[half, half],
        in_specs=[VMEM] * 6,
        out_specs=[VMEM] * 2,
        compiler_params=pltpu.CompilerParams(vmem_limit_bytes=16 * 2**20),
        cost_estimate=pl.CostEstimate(
            flops=4 * work * HD, bytes_accessed=4 * work, transcendentals=0
        ),
        name="query",
    )(ds_pair, behind_pair, here_pair, ds_own, behind, here)

    pieces = pl.pallas_call(
        functools.partial(total_kernel, groups),
        out_shape=[piece] * groups,
        in_specs=[VMEM] * 2,
        out_specs=[VMEM] * groups,
        compiler_params=SMALL,
        name="total",
    )(own, came_halo)
    returned = [pieces[0]] + [around(block, step) for step, block in enumerate(pieces[1:], 1)]
    attn_out, q_grad, filled = pl.pallas_call(
        fill_kernel,
        out_shape=[shape(queries.shape, bf)] * 2 + [shape((8, HD), jnp.float32)],
        in_specs=[VMEM] * 4 + [ANY],
        out_specs=[HBM, HBM, VMEM],
        scratch_shapes=[pltpu.SemaphoreType.DMA((4,))],
        compiler_params=SMALL,
        cost_estimate=pl.CostEstimate(
            flops=0, bytes_accessed=16 * side * width, transcendentals=0
        ),
        name="fill",
    )(attn_pair, attn_own, dq_pair, dq_own, returned[1])
    kept, for_pair = pl.pallas_call(
        functools.partial(place_kernel, groups),
        out_shape=[shape((2, rows, keys.shape[3]), bf)] * 2,
        in_specs=[VMEM] * groups + [ANY],
        out_specs=[VMEM] * 2,
        compiler_params=SMALL,
        name="place",
    )(*returned, filled)
    k_grad, v_grad = pl.pallas_call(
        finish_kernel,
        out_shape=[shape(keys.shape, bf)] * 2,
        in_specs=[VMEM] * 2,
        out_specs=[VMEM] * 2,
        compiler_params=SMALL,
        name="finish",
    )(kept, to_partner(for_pair))

    return (attn_out, q_grad, k_grad, v_grad)


def solution(mesh):
    heads, tokens = P(None, "cp", None, "tp"), P(None, "cp", "tp", None)
    return jax.shard_map(
        local,
        mesh=mesh,
        in_specs=(heads, tokens, tokens, heads, P()),
        out_specs=(heads, heads, tokens, tokens),
        check_vma=False,
    )
```

```python
import functools
import math

import jax
import jax.numpy as jnp
from jax import lax
from jax.experimental import pallas as pl
from jax.experimental.pallas import tpu as pltpu
from jax.sharding import PartitionSpec as P

HD = 128
FACTOR = 1.0 / math.sqrt(HD)
LOG2E = math.log2(math.e)
OUT = -1e30
VMEM = pl.BlockSpec(memory_space=pltpu.VMEM)
HBM = pl.BlockSpec(memory_space=pltpu.HBM)
ANY = pl.BlockSpec(memory_space=pl.ANY)
SMALL = pltpu.CompilerParams(vmem_limit_bytes=4 * 2**20)


def far_x(i, contexts):
    if i % 2:
        return i - 2
    return i + 2 if i + 2 < contexts else i + 1


def across_y(i, contexts):
    if i % 2:
        return min(i + 1, contexts - 1)
    return i - 1


def far_y(i, contexts):
    if i % 2:
        return i + 2 if i + 2 < contexts else i - 1
    return i - 2


def near_x(i, contexts):
    return i ^ 1


def move(block, target, back=False):
    contexts = lax.axis_size("cp")
    route = [(i, target(i, contexts)) for i in range(contexts) if target(i, contexts) >= 0]
    if back:
        route = [(there, here) for here, there in route]
    return lax.ppermute(block, "cp", route)


def offset(step, core, groups):
    return jnp.where(core == 0, step, groups - step)


def around(block, step):
    contexts, groups = lax.axis_size("cp"), lax.axis_size("tp")
    route = []
    for i in range(contexts):
        turn = step if i % 2 == 0 else groups - step
        route += [(i * groups + t, i * groups + (t + turn) % groups) for t in range(groups)]
    return lax.ppermute(block, ("cp", "tp"), route)


def dot(a, b, contract):
    return lax.dot_general(a, b, (contract, ((), ())), preferred_element_type=jnp.float32)


def aligned(index, size):
    return pl.ds(pl.multiple_of(index * size, size), size)


def split_kernel(groups, kv_ref, *pieces):
    tp, core = lax.axis_index("tp"), lax.rem(lax.axis_index("cp"), 2)
    for step, piece in enumerate(pieces, 1):
        lanes = aligned(lax.rem(tp + offset(step, core, groups), groups), HD)
        for kind in range(2):
            for block, half in enumerate((core, 1 - core)):
                piece[block, kind] = kv_ref[kind, half, 0, :, lanes]


def join_kernel(groups, kv_ref, *refs):
    pieces, outs = refs[:-3], refs[-2:]
    tp, core = lax.axis_index("tp"), lax.rem(lax.axis_index("cp"), 2)
    rows = kv_ref.shape[3]
    for kind in range(2):
        for half, out in zip((core, 1 - core), outs):
            out[kind, aligned(tp, rows), :] = kv_ref[kind, half, 0, :, aligned(tp, HD)]
    for step, piece in enumerate(pieces, 1):
        source = lax.rem(tp - offset(step, core, groups) + groups, groups)
        for block, out in enumerate(outs):
            out[:, aligned(source, rows), :] = piece[block]


def total_kernel(groups, *refs):
    terms, pieces = refs[:6], refs[6:]
    tp, core = lax.axis_index("tp"), lax.rem(lax.axis_index("cp"), 2)
    rows = pieces[0].shape[2]
    for step, piece in enumerate(pieces):
        place = aligned(lax.rem(tp + offset(step, core, groups), groups), rows)
        for block in range(2):
            own, *came = [ref[:, place, :] for ref in terms[3 * block : 3 * block + 3]]
            for term in came:
                own = own + term.astype(jnp.float32)
            piece[block] = own.astype(piece.dtype)


def place_kernel(groups, *refs):
    pieces, outs = refs[:-3], refs[-2:]
    tp, core = lax.axis_index("tp"), lax.rem(lax.axis_index("cp"), 2)
    for step, piece in enumerate(pieces):
        lanes = aligned(lax.rem(tp - offset(step, core, groups) + groups, groups), HD)
        for block, half in enumerate((core, 1 - core)):
            for kind, out in enumerate(outs):
                out[half, 0, :, lanes] = piece[block, kind]


def prepare_kernel(contexts, q_ref, g_ref, len_ref, qg_ref, bias_ref, sems):
    cp = lax.axis_index("cp")
    core = lax.rem(cp, 2)
    copies = []
    for kind, ref in enumerate((q_ref, g_ref)):
        for turn, half in enumerate((core, 1 - core)):
            copies.append(
                pltpu.make_async_copy(
                    ref.at[half, 0], qg_ref.at[kind, turn], sems.at[2 * kind + turn]
                )
            )
    for copy in copies:
        copy.start()

    bf = jnp.bfloat16
    side, docs = bias_ref.shape[1], len_ref.shape[1]
    up, back = cp, 2 * contexts - 1 - cp
    blocks = (jnp.where(core == 0, up, back), jnp.where(core == 0, back, up))
    lengths = jnp.broadcast_to(len_ref[...], (8, docs))
    before = lax.broadcasted_iota(jnp.int32, (docs, docs), 0)
    after = lax.broadcasted_iota(jnp.int32, (docs, docs), 1)
    upto = (before <= after).astype(jnp.float32).astype(bf)
    coarse = (lengths // 16).astype(jnp.float32).astype(bf)
    fine = (lengths % 16).astype(jnp.float32).astype(bf)
    over = ((1,), (0,))
    ends = (16.0 * dot(coarse, upto, over) + dot(fine, upto, over))[0:1, :]
    row = lax.broadcasted_iota(jnp.int32, (side, side), 0)
    column = lax.broadcasted_iota(jnp.int32, (side, side), 1)
    key = column.astype(jnp.float32)
    shared = jnp.where(column <= row, key, key - 2.0 * side)
    for turn, block in enumerate(blocks):
        first = block * side
        position = lax.broadcasted_iota(jnp.int32, (side, docs), 0) + first
        begins = jnp.where(ends <= position.astype(jnp.float32), ends, 0.0)
        begins = jnp.max(begins, axis=1, keepdims=True) - first.astype(jnp.float32)
        bias_ref[turn, :, :side] = jnp.where(shared >= begins, 0.0, OUT)
        bias_ref[turn, :, side:] = jnp.where(key - side >= begins, 0.0, OUT)

    for copy in copies:
        copy.wait()


def fill_kernel(*refs):
    parts, (after_ref, attn_ref, dq_ref, done_ref, sems) = refs[:4], refs[4:]
    core = lax.rem(lax.axis_index("cp"), 2)
    copies = []
    for kind, ref in enumerate((attn_ref, dq_ref)):
        for turn, half in enumerate((core, 1 - core)):
            n = 2 * kind + turn
            copies.append(pltpu.make_async_copy(parts[n], ref.at[half, 0], sems.at[n]))
    for copy in copies:
        copy.start()
    done_ref[...] = jnp.zeros_like(done_ref)
    for copy in copies:
        copy.wait()


def blend(field, side):
    low = side // 2
    row = lax.broadcasted_iota(jnp.int32, (low, low), 0)
    column = lax.broadcasted_iota(jnp.int32, (low, low), 1)
    causal = column <= row
    old, own = field[:, :side], field[:, 2 * side :]
    top = jnp.concatenate(
        [jnp.where(causal, own[:low, :low], old[:low, :low]), old[:low, low:]], axis=1
    )
    bottom = jnp.concatenate(
        [own[low:, :low], jnp.where(causal, own[low:, low:], old[low:, low:])], axis=1
    )
    shared = jnp.concatenate([top, bottom], axis=0)
    return jnp.concatenate([shared, field[:, side : 2 * side]], axis=1)


def unblend(field, side):
    low = side // 2
    row = lax.broadcasted_iota(jnp.int32, (low, low), 0)
    column = lax.broadcasted_iota(jnp.int32, (low, low), 1)
    causal = column <= row
    bf = jnp.bfloat16
    none = jnp.zeros((low, low), bf)
    a, d = field[:low, :low], field[low:, low : 2 * low]
    b, c = field[:low, low : 2 * low].astype(bf), field[low:, :low].astype(bf)
    a_own, a_old = jnp.where(causal, a, 0.0).astype(bf), jnp.where(causal, 0.0, a).astype(bf)
    d_own, d_old = jnp.where(causal, d, 0.0).astype(bf), jnp.where(causal, 0.0, d).astype(bf)
    old = jnp.concatenate(
        [jnp.concatenate([a_old, b], axis=1), jnp.concatenate([none, d_old], axis=1)], axis=0
    )
    own = jnp.concatenate(
        [jnp.concatenate([a_own, none], axis=1), jnp.concatenate([c, d_own], axis=1)], axis=0
    )
    return jnp.concatenate([old, field[:, side:].astype(bf), own], axis=1)


def attend_kernel(
    turn,
    qg_ref,
    oldest_ref,
    middle_ref,
    here_ref,
    bias_ref,
    attn_ref,
    ds_ref,
    to_oldest_ref,
    to_middle_ref,
    own_ref,
    kt_ref,
    vt_ref,
    dk_ref,
    dv_ref,
):
    side, heads = attn_ref.shape[0], ds_ref.shape[0]
    bf = jnp.bfloat16
    over, down = ((1,), (0,)), ((0,), (0,))
    keys, values = [
        jnp.concatenate([oldest_ref[kind], middle_ref[kind], here_ref[kind]], axis=0)
        for kind in range(2)
    ]
    kt_ref[...] = keys.T
    vt_ref[...] = values.T

    def lanes(head):
        return slice(head * HD, (head + 1) * HD)

    def products(head):
        q, g = qg_ref[0, turn, :, lanes(head)], qg_ref[1, turn, :, lanes(head)]
        return q, g, dot(q, kt_ref[...], over), dot(g, vt_ref[...], over)

    def softmax(scores):
        scaled = blend(scores, side) * (FACTOR * LOG2E) + bias_ref[turn]
        raised = jnp.exp2(scaled - jnp.max(scaled, axis=1, keepdims=True))
        return raised * (1.0 / jnp.sum(raised, axis=1, keepdims=True))

    def finish(head, q, g, probs_low, ds):
        ds_ref[head] = ds
        value_term, key_term = dot(g, probs_low, down), dot(q, ds, down)
        if head == 0:
            dv_ref[...], dk_ref[...] = value_term, key_term
        else:
            dv_ref[...] += value_term
            dk_ref[...] += key_term

    pending = None
    ahead = products(0)
    for head in range(heads):
        q, g, scores, dprobs = ahead
        if head + 1 < heads:
            ahead = products(head + 1)
        probs = softmax(scores)
        probs_low = unblend(probs, side)
        attn = dot(probs_low, values, over).astype(bf)
        attn_ref[:, lanes(head)] = attn
        if pending is not None:
            finish(*pending)
        delta = jnp.sum(attn.astype(jnp.float32) * g.astype(jnp.float32), axis=1, keepdims=True)
        ds = unblend(probs * (blend(dprobs, side) - delta), side)
        pending = (head, q, g, probs_low, ds)
    finish(*pending)
    for kind, (ref, factor) in enumerate(((dk_ref, FACTOR), (dv_ref, 1.0))):
        for n, out in enumerate((to_oldest_ref, to_middle_ref, own_ref)):
            term = ref[:, n * side : (n + 1) * side].T * factor
            out[kind] = term.astype(out.dtype)


def query_kernel(*refs):
    inputs, outs = refs[:-2], refs[-2:]
    for turn, out in enumerate(outs):
        ds_ref, *blocks = inputs[4 * turn : 4 * turn + 4]
        heads = ds_ref.shape[0]
        keys = jnp.concatenate([ref[0] for ref in blocks], axis=0)
        for head in range(heads):
            dq = dot(ds_ref[head], keys, ((1,), (0,))) * FACTOR
            out[:, head * HD : (head + 1) * HD] = dq.astype(out.dtype)


def local(queries, keys, values, out_grad, doc_lengths):
    side, width = queries.shape[2], queries.shape[3]
    contexts, groups = lax.axis_size("cp"), lax.axis_size("tp")
    rows = keys.shape[2]
    bf = jnp.bfloat16
    shape = jax.ShapeDtypeStruct
    piece = shape((2, 2, rows, HD), bf)

    kv = jnp.stack([keys, values])
    sent = pl.pallas_call(
        functools.partial(split_kernel, groups),
        out_shape=[piece] * (groups - 1),
        in_specs=[VMEM],
        out_specs=[VMEM] * (groups - 1),
        compiler_params=SMALL,
        name="split",
    )(kv)
    came = [around(block, step) for step, block in enumerate(sent, 1)]
    qg, bias = pl.pallas_call(
        functools.partial(prepare_kernel, contexts),
        out_shape=[shape((2, 2, side, width), bf), shape((2, side, 2 * side), jnp.float32)],
        in_specs=[HBM, HBM, VMEM],
        out_specs=[VMEM] * 2,
        scratch_shapes=[pltpu.SemaphoreType.DMA((4,))],
        compiler_params=SMALL,
        cost_estimate=pl.CostEstimate(
            flops=0, bytes_accessed=16 * side * width, transcendentals=0
        ),
        name="prepare",
    )(queries, out_grad, doc_lengths[None, :])
    block = shape((2, side, HD), bf)
    x, y = pl.pallas_call(
        functools.partial(join_kernel, groups),
        out_shape=[block] * 2,
        in_specs=[VMEM] * groups + [ANY],
        out_specs=[VMEM] * 2,
        compiler_params=SMALL,
        name="join",
    )(kv, *came, bias)
    x_line = (move(x, far_x), move(y, across_y), x)
    y_line = (move(y, far_y), move(x, near_x), y)

    heads = width // HD
    work = heads * side * 3 * side
    half = shape((side, width), bf)

    def attend(turn, *line):
        return pl.pallas_call(
            functools.partial(attend_kernel, turn),
            in_specs=[VMEM] * 5,
            out_specs=[VMEM] * 5,
            scratch_shapes=[pltpu.VMEM((HD, 3 * side), bf)] * 2
            + [pltpu.VMEM((HD, 3 * side), jnp.float32)] * 2,
            out_shape=[
                half,
                shape((heads, side, 3 * side), bf),
                block,
                block,
                shape((2, side, HD), jnp.float32),
            ],
            compiler_params=pltpu.CompilerParams(vmem_limit_bytes=32 * 2**20),
            cost_estimate=pl.CostEstimate(
                flops=10 * work * HD, bytes_accessed=6 * side * width, transcendentals=work
            ),
            name="attend",
        )(qg, *line, bias)

    attn_x, ds_x, to_far_x, to_across_y, own_x = attend(0, *x_line)
    attn_y, ds_y, to_far_y, to_near_x, own_y = attend(1, *y_line)
    terms = (
        own_x,
        move(to_far_x, far_x, back=True),
        move(to_near_x, near_x, back=True),
        own_y,
        move(to_across_y, across_y, back=True),
        move(to_far_y, far_y, back=True),
    )
    dq_x, dq_y = pl.pallas_call(
        query_kernel,
        out_shape=[half, half],
        in_specs=[VMEM] * 8,
        out_specs=[VMEM] * 2,
        compiler_params=pltpu.CompilerParams(vmem_limit_bytes=16 * 2**20),
        cost_estimate=pl.CostEstimate(
            flops=4 * work * HD, bytes_accessed=4 * work, transcendentals=0
        ),
        name="query",
    )(ds_x, *x_line, ds_y, *y_line)

    pieces = pl.pallas_call(
        functools.partial(total_kernel, groups),
        out_shape=[piece] * groups,
        in_specs=[VMEM] * 6,
        out_specs=[VMEM] * groups,
        compiler_params=SMALL,
        name="total",
    )(*terms)
    returned = [pieces[0]] + [around(block, step) for step, block in enumerate(pieces[1:], 1)]
    attn_out, q_grad, filled = pl.pallas_call(
        fill_kernel,
        out_shape=[shape(queries.shape, bf)] * 2 + [shape((8, HD), jnp.float32)],
        in_specs=[VMEM] * 4 + [ANY],
        out_specs=[HBM, HBM, VMEM],
        scratch_shapes=[pltpu.SemaphoreType.DMA((4,))],
        compiler_params=SMALL,
        cost_estimate=pl.CostEstimate(
            flops=0, bytes_accessed=16 * side * width, transcendentals=0
        ),
        name="fill",
    )(attn_x, attn_y, dq_x, dq_y, returned[1])
    k_grad, v_grad = pl.pallas_call(
        functools.partial(place_kernel, groups),
        out_shape=[shape(keys.shape, bf)] * 2,
        in_specs=[VMEM] * groups + [ANY],
        out_specs=[VMEM] * 2,
        compiler_params=SMALL,
        name="place",
    )(*returned, filled)
    return (attn_out, q_grad, k_grad, v_grad)


def solution(mesh):
    heads, tokens = P(None, "cp", None, "tp"), P(None, "cp", "tp", None)
    return jax.shard_map(
        local,
        mesh=mesh,
        in_specs=(heads, tokens, tokens, heads, P()),
        out_specs=(heads, heads, tokens, tokens),
        check_vma=False,
    )
```

```python
import functools
import math

import jax
import jax.numpy as jnp
from jax import lax
from jax.experimental import pallas as pl
from jax.experimental.pallas import tpu as pltpu
from jax.sharding import PartitionSpec as P

HD = 128
FACTOR = 1.0 / math.sqrt(HD)
LOG2E = math.log2(math.e)
OUT = -1e30
VMEM = pl.BlockSpec(memory_space=pltpu.VMEM)
HBM = pl.BlockSpec(memory_space=pltpu.HBM)
ANY = pl.BlockSpec(memory_space=pl.ANY)
SMALL = pltpu.CompilerParams(vmem_limit_bytes=4 * 2**20)


def far_x(i, contexts):
    if i % 2:
        return i - 2
    return i + 2 if i + 2 < contexts else i + 1


def far_y(i, contexts):
    if i % 2:
        return i + 2 if i + 2 < contexts else i - 1
    return i - 2


def partner(i, contexts):
    return i ^ 1


def move(block, target, back=False):
    contexts = lax.axis_size("cp")
    route = [(i, target(i, contexts)) for i in range(contexts) if target(i, contexts) >= 0]
    if back:
        route = [(there, here) for here, there in route]
    return lax.ppermute(block, "cp", route)


def offset(step, core, groups):
    return jnp.where(core == 0, step, groups - step)


def around(block, step):
    contexts, groups = lax.axis_size("cp"), lax.axis_size("tp")
    route = []
    for i in range(contexts):
        turn = step if i % 2 == 0 else groups - step
        route += [(i * groups + t, i * groups + (t + turn) % groups) for t in range(groups)]
    return lax.ppermute(block, ("cp", "tp"), route)


def dot(a, b, contract):
    return lax.dot_general(a, b, (contract, ((), ())), preferred_element_type=jnp.float32)


def aligned(index, size):
    return pl.ds(pl.multiple_of(index * size, size), size)


def split_kernel(groups, kv_ref, *pieces):
    tp, core = lax.axis_index("tp"), lax.rem(lax.axis_index("cp"), 2)
    for step, piece in enumerate(pieces, 1):
        lanes = aligned(lax.rem(tp + offset(step, core, groups), groups), HD)
        for kind in range(2):
            for block, half in enumerate((core, 1 - core)):
                piece[block, kind] = kv_ref[kind, half, 0, :, lanes]


def join_kernel(groups, kv_ref, *refs):
    pieces, outs = refs[:-3], refs[-2:]
    tp, core = lax.axis_index("tp"), lax.rem(lax.axis_index("cp"), 2)
    rows = kv_ref.shape[3]
    for kind in range(2):
        for half, out in zip((core, 1 - core), outs):
            out[kind, aligned(tp, rows), :] = kv_ref[kind, half, 0, :, aligned(tp, HD)]
    for step, piece in enumerate(pieces, 1):
        source = lax.rem(tp - offset(step, core, groups) + groups, groups)
        for block, out in enumerate(outs):
            out[:, aligned(source, rows), :] = piece[block]


def both_kernel(x_ref, came_ref, after_ref, out_ref):
    out_ref[0] = x_ref[...]
    out_ref[1] = came_ref[...]


def total_kernel(groups, *refs):
    terms, pieces = (refs[:3], refs[3:5]), refs[5:]
    tp, core = lax.axis_index("tp"), lax.rem(lax.axis_index("cp"), 2)
    rows = pieces[0].shape[2]
    for step, piece in enumerate(pieces):
        place = aligned(lax.rem(tp + offset(step, core, groups), groups), rows)
        for block in range(2):
            own, *came = [ref[:, place, :] for ref in terms[block]]
            for term in came:
                own = own + term.astype(jnp.float32)
            piece[block] = own.astype(piece.dtype)


def place_kernel(groups, *refs):
    pieces, outs = refs[:-3], refs[-2:]
    tp, core = lax.axis_index("tp"), lax.rem(lax.axis_index("cp"), 2)
    for step, piece in enumerate(pieces):
        lanes = aligned(lax.rem(tp - offset(step, core, groups) + groups, groups), HD)
        for block, half in enumerate((core, 1 - core)):
            for kind, out in enumerate(outs):
                out[half, 0, :, lanes] = piece[block, kind]


def prepare_kernel(contexts, q_ref, g_ref, len_ref, qg_ref, bias_ref, sems):
    cp = lax.axis_index("cp")
    core = lax.rem(cp, 2)
    copies = []
    for kind, ref in enumerate((q_ref, g_ref)):
        for turn, half in enumerate((core, 1 - core)):
            copies.append(
                pltpu.make_async_copy(
                    ref.at[half, 0], qg_ref.at[kind, turn], sems.at[2 * kind + turn]
                )
            )
    for copy in copies:
        copy.start()

    bf = jnp.bfloat16
    side, docs = bias_ref.shape[1], len_ref.shape[1]
    up, back = cp, 2 * contexts - 1 - cp
    blocks = (jnp.where(core == 0, up, back), jnp.where(core == 0, back, up))
    lengths = jnp.broadcast_to(len_ref[...], (8, docs))
    before = lax.broadcasted_iota(jnp.int32, (docs, docs), 0)
    after = lax.broadcasted_iota(jnp.int32, (docs, docs), 1)
    upto = (before <= after).astype(jnp.float32).astype(bf)
    coarse = (lengths // 16).astype(jnp.float32).astype(bf)
    fine = (lengths % 16).astype(jnp.float32).astype(bf)
    over = ((1,), (0,))
    ends = (16.0 * dot(coarse, upto, over) + dot(fine, upto, over))[0:1, :]
    row = lax.broadcasted_iota(jnp.int32, (side, side), 0)
    column = lax.broadcasted_iota(jnp.int32, (side, side), 1)
    key = column.astype(jnp.float32)
    shared = jnp.where(column <= row, key, key - 2.0 * side)
    for turn, block in enumerate(blocks):
        first = block * side
        position = lax.broadcasted_iota(jnp.int32, (side, docs), 0) + first
        begins = jnp.where(ends <= position.astype(jnp.float32), ends, 0.0)
        begins = jnp.max(begins, axis=1, keepdims=True) - first.astype(jnp.float32)
        bias_ref[turn, :, :side] = jnp.where(shared >= begins, 0.0, OUT)
        bias_ref[turn, :, side:] = jnp.where(key - side >= begins, 0.0, OUT)

    for copy in copies:
        copy.wait()


def fill_kernel(*refs):
    parts, (after_ref, attn_ref, dq_ref, done_ref, sems) = refs[:4], refs[4:]
    core = lax.rem(lax.axis_index("cp"), 2)
    copies = []
    for kind, ref in enumerate((attn_ref, dq_ref)):
        for turn, half in enumerate((core, 1 - core)):
            n = 2 * kind + turn
            copies.append(pltpu.make_async_copy(parts[n], ref.at[half, 0], sems.at[n]))
    for copy in copies:
        copy.start()
    done_ref[...] = jnp.zeros_like(done_ref)
    for copy in copies:
        copy.wait()


def blend(field, side):
    low = side // 2
    row = lax.broadcasted_iota(jnp.int32, (low, low), 0)
    column = lax.broadcasted_iota(jnp.int32, (low, low), 1)
    causal = column <= row
    old, own = field[:, :side], field[:, 2 * side :]
    top = jnp.concatenate(
        [jnp.where(causal, own[:low, :low], old[:low, :low]), old[:low, low:]], axis=1
    )
    bottom = jnp.concatenate(
        [own[low:, :low], jnp.where(causal, own[low:, low:], old[low:, low:])], axis=1
    )
    shared = jnp.concatenate([top, bottom], axis=0)
    return jnp.concatenate([shared, field[:, side : 2 * side]], axis=1)


def unblend(field, side):
    low = side // 2
    row = lax.broadcasted_iota(jnp.int32, (low, low), 0)
    column = lax.broadcasted_iota(jnp.int32, (low, low), 1)
    causal = column <= row
    bf = jnp.bfloat16
    none = jnp.zeros((low, low), bf)
    a, d = field[:low, :low], field[low:, low : 2 * low]
    b, c = field[:low, low : 2 * low].astype(bf), field[low:, :low].astype(bf)
    a_own, a_old = jnp.where(causal, a, 0.0).astype(bf), jnp.where(causal, 0.0, a).astype(bf)
    d_own, d_old = jnp.where(causal, d, 0.0).astype(bf), jnp.where(causal, 0.0, d).astype(bf)
    old = jnp.concatenate(
        [jnp.concatenate([a_old, b], axis=1), jnp.concatenate([none, d_old], axis=1)], axis=0
    )
    own = jnp.concatenate(
        [jnp.concatenate([a_own, none], axis=1), jnp.concatenate([c, d_own], axis=1)], axis=0
    )
    return jnp.concatenate([old, field[:, side:].astype(bf), own], axis=1)


def window(turn, kind, oldest_ref, shared_ref, here_ref):
    return jnp.concatenate(
        [oldest_ref[kind], shared_ref[1 - turn, kind], here_ref[kind]], axis=0
    )


def attend_kernel(turn, qg_ref, oldest_ref, shared_ref, here_ref, bias_ref, *refs):
    if turn == 0:
        more_ref = None
    else:
        more_ref, *refs = refs
    attn_ref, ds_ref, to_oldest_ref, to_middle_ref, own_ref, kt_ref, vt_ref, dk_ref, dv_ref = refs
    side, heads = attn_ref.shape[0], ds_ref.shape[0]
    bf = jnp.bfloat16
    over, down = ((1,), (0,)), ((0,), (0,))
    keys, values = [window(turn, kind, oldest_ref, shared_ref, here_ref) for kind in range(2)]
    kt_ref[...] = keys.T
    vt_ref[...] = values.T

    def lanes(head):
        return slice(head * HD, (head + 1) * HD)

    def products(head):
        q, g = qg_ref[0, turn, :, lanes(head)], qg_ref[1, turn, :, lanes(head)]
        return q, g, dot(q, kt_ref[...], over), dot(g, vt_ref[...], over)

    def softmax(scores):
        scaled = blend(scores, side) * (FACTOR * LOG2E) + bias_ref[turn]
        raised = jnp.exp2(scaled - jnp.max(scaled, axis=1, keepdims=True))
        return raised * (1.0 / jnp.sum(raised, axis=1, keepdims=True))

    def finish(head, q, g, probs_low, ds):
        ds_ref[head] = ds
        value_term, key_term = dot(g, probs_low, down), dot(q, ds, down)
        if head == 0:
            dv_ref[...], dk_ref[...] = value_term, key_term
        else:
            dv_ref[...] += value_term
            dk_ref[...] += key_term

    pending = None
    ahead = products(0)
    for head in range(heads):
        q, g, scores, dprobs = ahead
        if head + 1 < heads:
            ahead = products(head + 1)
        probs = softmax(scores)
        probs_low = unblend(probs, side)
        attn = dot(probs_low, values, over).astype(bf)
        attn_ref[:, lanes(head)] = attn
        if pending is not None:
            finish(*pending)
        delta = jnp.sum(attn.astype(jnp.float32) * g.astype(jnp.float32), axis=1, keepdims=True)
        ds = unblend(probs * (blend(dprobs, side) - delta), side)
        pending = (head, q, g, probs_low, ds)
    finish(*pending)
    for kind, (ref, factor) in enumerate(((dk_ref, FACTOR), (dv_ref, 1.0))):
        for n, out in enumerate((to_oldest_ref, to_middle_ref, own_ref)):
            term = ref[:, n * side : (n + 1) * side].T * factor
            if n == 0 and more_ref is not None:
                term = term + more_ref[kind].astype(jnp.float32)
            out[kind] = term.astype(out.dtype)


def query_kernel(*refs):
    inputs, outs = refs[:-2], refs[-2:]
    for turn, out in enumerate(outs):
        ds_ref, *line = inputs[4 * turn : 4 * turn + 4]
        heads = ds_ref.shape[0]
        keys = window(turn, 0, *line)
        for head in range(heads):
            dq = dot(ds_ref[head], keys, ((1,), (0,))) * FACTOR
            out[:, head * HD : (head + 1) * HD] = dq.astype(out.dtype)


def local(queries, keys, values, out_grad, doc_lengths):
    side, width = queries.shape[2], queries.shape[3]
    contexts, groups = lax.axis_size("cp"), lax.axis_size("tp")
    rows = keys.shape[2]
    bf = jnp.bfloat16
    shape = jax.ShapeDtypeStruct
    piece = shape((2, 2, rows, HD), bf)

    kv = jnp.stack([keys, values])
    sent = pl.pallas_call(
        functools.partial(split_kernel, groups),
        out_shape=[piece] * (groups - 1),
        in_specs=[VMEM],
        out_specs=[VMEM] * (groups - 1),
        compiler_params=SMALL,
        name="split",
    )(kv)
    came = [around(block, step) for step, block in enumerate(sent, 1)]
    qg, bias = pl.pallas_call(
        functools.partial(prepare_kernel, contexts),
        out_shape=[shape((2, 2, side, width), bf), shape((2, side, 2 * side), jnp.float32)],
        in_specs=[HBM, HBM, VMEM],
        out_specs=[VMEM] * 2,
        scratch_shapes=[pltpu.SemaphoreType.DMA((4,))],
        compiler_params=SMALL,
        cost_estimate=pl.CostEstimate(
            flops=0, bytes_accessed=16 * side * width, transcendentals=0
        ),
        name="prepare",
    )(queries, out_grad, doc_lengths[None, :])
    block = shape((2, side, HD), bf)
    x, y = pl.pallas_call(
        functools.partial(join_kernel, groups),
        out_shape=[block] * 2,
        in_specs=[VMEM] * groups + [ANY],
        out_specs=[VMEM] * 2,
        compiler_params=SMALL,
        name="join",
    )(kv, *came, bias)
    came_y, came_x = move(y, far_y), move(x, far_x)
    both = pl.pallas_call(
        both_kernel,
        out_shape=shape((2, 2, side, HD), bf),
        in_specs=[VMEM, VMEM, ANY],
        out_specs=VMEM,
        compiler_params=SMALL,
        name="both",
    )(x, came_y, came_x)
    shared = move(both, partner)
    x_line = (came_x, shared, x)
    y_line = (came_y, shared, y)

    heads = width // HD
    work = heads * side * 3 * side
    half = shape((side, width), bf)

    def attend(turn, line, *more):
        return pl.pallas_call(
            functools.partial(attend_kernel, turn),
            in_specs=[VMEM] * (5 + len(more)),
            out_specs=[VMEM] * 5,
            scratch_shapes=[pltpu.VMEM((HD, 3 * side), bf)] * 2
            + [pltpu.VMEM((HD, 3 * side), jnp.float32)] * 2,
            out_shape=[
                half,
                shape((heads, side, 3 * side), bf),
                block,
                block,
                shape((2, side, HD), jnp.float32),
            ],
            compiler_params=pltpu.CompilerParams(vmem_limit_bytes=32 * 2**20),
            cost_estimate=pl.CostEstimate(
                flops=10 * work * HD, bytes_accessed=6 * side * width, transcendentals=work
            ),
            name="attend",
        )(qg, *line, bias, *more)

    attn_x, ds_x, for_far_x, for_partner, own_x = attend(0, x_line)
    more = move(for_partner, partner, back=True)
    from_far_x = move(for_far_x, far_x, back=True)
    attn_y, ds_y, for_far_y, for_partner, own_y = attend(1, y_line, more)
    terms = (
        (own_x, from_far_x, move(for_partner, partner, back=True)),
        (own_y, move(for_far_y, far_y, back=True)),
    )
    dq_x, dq_y = pl.pallas_call(
        query_kernel,
        out_shape=[half, half],
        in_specs=[VMEM] * 8,
        out_specs=[VMEM] * 2,
        compiler_params=pltpu.CompilerParams(vmem_limit_bytes=16 * 2**20),
        cost_estimate=pl.CostEstimate(
            flops=4 * work * HD, bytes_accessed=4 * work, transcendentals=0
        ),
        name="query",
    )(ds_x, *x_line, ds_y, *y_line)

    pieces = pl.pallas_call(
        functools.partial(total_kernel, groups),
        out_shape=[piece] * groups,
        in_specs=[VMEM] * 5,
        out_specs=[VMEM] * groups,
        compiler_params=SMALL,
        name="total",
    )(*terms[0], *terms[1])
    returned = [pieces[0]] + [around(block, step) for step, block in enumerate(pieces[1:], 1)]
    attn_out, q_grad, filled = pl.pallas_call(
        fill_kernel,
        out_shape=[shape(queries.shape, bf)] * 2 + [shape((8, HD), jnp.float32)],
        in_specs=[VMEM] * 4 + [ANY],
        out_specs=[HBM, HBM, VMEM],
        scratch_shapes=[pltpu.SemaphoreType.DMA((4,))],
        compiler_params=SMALL,
        cost_estimate=pl.CostEstimate(
            flops=0, bytes_accessed=16 * side * width, transcendentals=0
        ),
        name="fill",
    )(attn_x, attn_y, dq_x, dq_y, returned[1])
    k_grad, v_grad = pl.pallas_call(
        functools.partial(place_kernel, groups),
        out_shape=[shape(keys.shape, bf)] * 2,
        in_specs=[VMEM] * groups + [ANY],
        out_specs=[VMEM] * 2,
        compiler_params=SMALL,
        name="place",
    )(*returned, filled)
    return (attn_out, q_grad, k_grad, v_grad)


def solution(mesh):
    heads, tokens = P(None, "cp", None, "tp"), P(None, "cp", "tp", None)
    return jax.shard_map(
        local,
        mesh=mesh,
        in_specs=(heads, tokens, tokens, heads, P()),
        out_specs=(heads, heads, tokens, tokens),
        check_vma=False,
    )
```

```python
import functools
import math

import jax
import jax.numpy as jnp
from jax import lax
from jax.experimental import pallas as pl
from jax.experimental.pallas import tpu as pltpu
from jax.sharding import PartitionSpec as P

HD = 128
FACTOR = 1.0 / math.sqrt(HD)
LOG2E = math.log2(math.e)
OUT = -1e30
VMEM = pl.BlockSpec(memory_space=pltpu.VMEM)
HBM = pl.BlockSpec(memory_space=pltpu.HBM)
ANY = pl.BlockSpec(memory_space=pl.ANY)
SMALL = pltpu.CompilerParams(vmem_limit_bytes=4 * 2**20)


def far_x(i, contexts):
    if i % 2:
        return i - 2
    return i + 2 if i + 2 < contexts else i + 1


def across_y(i, contexts):
    if i % 2:
        return min(i + 1, contexts - 1)
    return i - 1


def far_y(i, contexts):
    if i % 2:
        return i + 2 if i + 2 < contexts else i - 1
    return i - 2


def partner(i, contexts):
    return i ^ 1


def move(block, target, back=False):
    contexts = lax.axis_size("cp")
    route = [(i, target(i, contexts)) for i in range(contexts) if target(i, contexts) >= 0]
    if back:
        route = [(there, here) for here, there in route]
    return lax.ppermute(block, "cp", route)


def offset(step, core, groups):
    return jnp.where(core == 0, step, groups - step)


def around(block, step):
    contexts, groups = lax.axis_size("cp"), lax.axis_size("tp")
    route = []
    for i in range(contexts):
        turn = step if i % 2 == 0 else groups - step
        route += [(i * groups + t, i * groups + (t + turn) % groups) for t in range(groups)]
    return lax.ppermute(block, ("cp", "tp"), route)


def dot(a, b, contract):
    return lax.dot_general(a, b, (contract, ((), ())), preferred_element_type=jnp.float32)


def aligned(index, size):
    return pl.ds(pl.multiple_of(index * size, size), size)


def split_kernel(groups, kv_ref, *pieces):
    tp, core = lax.axis_index("tp"), lax.rem(lax.axis_index("cp"), 2)
    for step, piece in enumerate(pieces, 1):
        lanes = aligned(lax.rem(tp + offset(step, core, groups), groups), HD)
        for kind in range(2):
            for block, half in enumerate((core, 1 - core)):
                piece[block, kind] = kv_ref[kind, half, 0, :, lanes]


def join_kernel(groups, kv_ref, *refs):
    pieces, outs = refs[:-3], refs[-2:]
    tp, core = lax.axis_index("tp"), lax.rem(lax.axis_index("cp"), 2)
    rows = kv_ref.shape[3]
    for kind in range(2):
        for half, out in zip((core, 1 - core), outs):
            out[kind, aligned(tp, rows), :] = kv_ref[kind, half, 0, :, aligned(tp, HD)]
    for step, piece in enumerate(pieces, 1):
        source = lax.rem(tp - offset(step, core, groups) + groups, groups)
        for block, out in enumerate(outs):
            out[:, aligned(source, rows), :] = piece[block]


def total_kernel(groups, *refs):
    terms, pieces = (refs[:3], refs[3:5]), refs[5:]
    tp, core = lax.axis_index("tp"), lax.rem(lax.axis_index("cp"), 2)
    rows = pieces[0].shape[2]
    for step, piece in enumerate(pieces):
        place = aligned(lax.rem(tp + offset(step, core, groups), groups), rows)
        for block in range(2):
            own, *came = [ref[:, place, :] for ref in terms[block]]
            for term in came:
                own = own + term.astype(jnp.float32)
            piece[block] = own.astype(piece.dtype)


def place_kernel(groups, *refs):
    pieces, outs = refs[:-3], refs[-2:]
    tp, core = lax.axis_index("tp"), lax.rem(lax.axis_index("cp"), 2)
    for step, piece in enumerate(pieces):
        lanes = aligned(lax.rem(tp - offset(step, core, groups) + groups, groups), HD)
        for block, half in enumerate((core, 1 - core)):
            for kind, out in enumerate(outs):
                out[half, 0, :, lanes] = piece[block, kind]


def prepare_kernel(contexts, q_ref, g_ref, len_ref, qg_ref, bias_ref, sems):
    cp = lax.axis_index("cp")
    core = lax.rem(cp, 2)
    copies = []
    for kind, ref in enumerate((q_ref, g_ref)):
        for turn, half in enumerate((core, 1 - core)):
            copies.append(
                pltpu.make_async_copy(
                    ref.at[half, 0], qg_ref.at[kind, turn], sems.at[2 * kind + turn]
                )
            )
    for copy in copies:
        copy.start()

    bf = jnp.bfloat16
    side, docs = bias_ref.shape[1], len_ref.shape[1]
    up, back = cp, 2 * contexts - 1 - cp
    blocks = (jnp.where(core == 0, up, back), jnp.where(core == 0, back, up))
    lengths = jnp.broadcast_to(len_ref[...], (8, docs))
    before = lax.broadcasted_iota(jnp.int32, (docs, docs), 0)
    after = lax.broadcasted_iota(jnp.int32, (docs, docs), 1)
    upto = (before <= after).astype(jnp.float32).astype(bf)
    coarse = (lengths // 16).astype(jnp.float32).astype(bf)
    fine = (lengths % 16).astype(jnp.float32).astype(bf)
    over = ((1,), (0,))
    ends = (16.0 * dot(coarse, upto, over) + dot(fine, upto, over))[0:1, :]
    row = lax.broadcasted_iota(jnp.int32, (side, side), 0)
    column = lax.broadcasted_iota(jnp.int32, (side, side), 1)
    key = column.astype(jnp.float32)
    shared = jnp.where(column <= row, key, key - 2.0 * side)
    for turn, block in enumerate(blocks):
        first = block * side
        position = lax.broadcasted_iota(jnp.int32, (side, docs), 0) + first
        begins = jnp.where(ends <= position.astype(jnp.float32), ends, 0.0)
        begins = jnp.max(begins, axis=1, keepdims=True) - first.astype(jnp.float32)
        bias_ref[turn, :, :side] = jnp.where(shared >= begins, 0.0, OUT)
        bias_ref[turn, :, side:] = jnp.where(key - side >= begins, 0.0, OUT)

    for copy in copies:
        copy.wait()


def fill_kernel(*refs):
    parts, (after_ref, attn_ref, dq_ref, done_ref, sems) = refs[:4], refs[4:]
    core = lax.rem(lax.axis_index("cp"), 2)
    copies = []
    for kind, ref in enumerate((attn_ref, dq_ref)):
        for turn, half in enumerate((core, 1 - core)):
            n = 2 * kind + turn
            copies.append(pltpu.make_async_copy(parts[n], ref.at[half, 0], sems.at[n]))
    for copy in copies:
        copy.start()
    done_ref[...] = jnp.zeros_like(done_ref)
    for copy in copies:
        copy.wait()


def blend(field, side):
    low = side // 2
    row = lax.broadcasted_iota(jnp.int32, (low, low), 0)
    column = lax.broadcasted_iota(jnp.int32, (low, low), 1)
    causal = column <= row
    old, own = field[:, :side], field[:, 2 * side :]
    top = jnp.concatenate(
        [jnp.where(causal, own[:low, :low], old[:low, :low]), old[:low, low:]], axis=1
    )
    bottom = jnp.concatenate(
        [own[low:, :low], jnp.where(causal, own[low:, low:], old[low:, low:])], axis=1
    )
    shared = jnp.concatenate([top, bottom], axis=0)
    return jnp.concatenate([shared, field[:, side : 2 * side]], axis=1)


def unblend(field, side):
    low = side // 2
    row = lax.broadcasted_iota(jnp.int32, (low, low), 0)
    column = lax.broadcasted_iota(jnp.int32, (low, low), 1)
    causal = column <= row
    bf = jnp.bfloat16
    none = jnp.zeros((low, low), bf)
    a, d = field[:low, :low], field[low:, low : 2 * low]
    b, c = field[:low, low : 2 * low].astype(bf), field[low:, :low].astype(bf)
    a_own, a_old = jnp.where(causal, a, 0.0).astype(bf), jnp.where(causal, 0.0, a).astype(bf)
    d_own, d_old = jnp.where(causal, d, 0.0).astype(bf), jnp.where(causal, 0.0, d).astype(bf)
    old = jnp.concatenate(
        [jnp.concatenate([a_old, b], axis=1), jnp.concatenate([none, d_old], axis=1)], axis=0
    )
    own = jnp.concatenate(
        [jnp.concatenate([a_own, none], axis=1), jnp.concatenate([c, d_own], axis=1)], axis=0
    )
    return jnp.concatenate([old, field[:, side:].astype(bf), own], axis=1)


def window(kind, *line):
    return jnp.concatenate([ref[kind] for ref in line], axis=0)


def attend_kernel(turn, qg_ref, oldest_ref, middle_ref, here_ref, bias_ref, *refs):
    if turn == 0:
        more_ref = None
    else:
        more_ref, *refs = refs
    attn_ref, ds_ref, to_oldest_ref, to_middle_ref, own_ref, kt_ref, vt_ref, dk_ref, dv_ref = refs
    side, heads = attn_ref.shape[0], ds_ref.shape[0]
    bf = jnp.bfloat16
    over, down = ((1,), (0,)), ((0,), (0,))
    keys, values = [window(kind, oldest_ref, middle_ref, here_ref) for kind in range(2)]
    kt_ref[...] = keys.T
    vt_ref[...] = values.T

    def lanes(head):
        return slice(head * HD, (head + 1) * HD)

    def products(head):
        q, g = qg_ref[0, turn, :, lanes(head)], qg_ref[1, turn, :, lanes(head)]
        return q, g, dot(q, kt_ref[...], over), dot(g, vt_ref[...], over)

    def softmax(scores):
        scaled = blend(scores, side) * (FACTOR * LOG2E) + bias_ref[turn]
        raised = jnp.exp2(scaled - jnp.max(scaled, axis=1, keepdims=True))
        return raised * (1.0 / jnp.sum(raised, axis=1, keepdims=True))

    def finish(head, q, g, probs_low, ds):
        ds_ref[head] = ds
        value_term, key_term = dot(g, probs_low, down), dot(q, ds, down)
        if head == 0:
            dv_ref[...], dk_ref[...] = value_term, key_term
        else:
            dv_ref[...] += value_term
            dk_ref[...] += key_term

    pending = None
    ahead = products(0)
    for head in range(heads):
        q, g, scores, dprobs = ahead
        if head + 1 < heads:
            ahead = products(head + 1)
        probs = softmax(scores)
        probs_low = unblend(probs, side)
        attn = dot(probs_low, values, over).astype(bf)
        attn_ref[:, lanes(head)] = attn
        if pending is not None:
            finish(*pending)
        delta = jnp.sum(attn.astype(jnp.float32) * g.astype(jnp.float32), axis=1, keepdims=True)
        ds = unblend(probs * (blend(dprobs, side) - delta), side)
        pending = (head, q, g, probs_low, ds)
    finish(*pending)
    for kind, (ref, factor) in enumerate(((dk_ref, FACTOR), (dv_ref, 1.0))):
        for n, out in enumerate((to_oldest_ref, to_middle_ref, own_ref)):
            term = ref[:, n * side : (n + 1) * side].T * factor
            if n == 0 and more_ref is not None:
                term = term + more_ref[kind].astype(jnp.float32)
            out[kind] = term.astype(out.dtype)


def query_kernel(*refs):
    inputs, outs = refs[:-2], refs[-2:]
    for turn, out in enumerate(outs):
        ds_ref, *line = inputs[4 * turn : 4 * turn + 4]
        heads = ds_ref.shape[0]
        keys = window(0, *line)
        for head in range(heads):
            dq = dot(ds_ref[head], keys, ((1,), (0,))) * FACTOR
            out[:, head * HD : (head + 1) * HD] = dq.astype(out.dtype)


def local(queries, keys, values, out_grad, doc_lengths):
    side, width = queries.shape[2], queries.shape[3]
    contexts, groups = lax.axis_size("cp"), lax.axis_size("tp")
    rows = keys.shape[2]
    bf = jnp.bfloat16
    shape = jax.ShapeDtypeStruct
    piece = shape((2, 2, rows, HD), bf)

    kv = jnp.stack([keys, values])
    sent = pl.pallas_call(
        functools.partial(split_kernel, groups),
        out_shape=[piece] * (groups - 1),
        in_specs=[VMEM],
        out_specs=[VMEM] * (groups - 1),
        compiler_params=SMALL,
        name="split",
    )(kv)
    came = [around(block, step) for step, block in enumerate(sent, 1)]
    qg, bias = pl.pallas_call(
        functools.partial(prepare_kernel, contexts),
        out_shape=[shape((2, 2, side, width), bf), shape((2, side, 2 * side), jnp.float32)],
        in_specs=[HBM, HBM, VMEM],
        out_specs=[VMEM] * 2,
        scratch_shapes=[pltpu.SemaphoreType.DMA((4,))],
        compiler_params=SMALL,
        cost_estimate=pl.CostEstimate(
            flops=0, bytes_accessed=16 * side * width, transcendentals=0
        ),
        name="prepare",
    )(queries, out_grad, doc_lengths[None, :])
    block = shape((2, side, HD), bf)
    x, y = pl.pallas_call(
        functools.partial(join_kernel, groups),
        out_shape=[block] * 2,
        in_specs=[VMEM] * groups + [ANY],
        out_specs=[VMEM] * 2,
        compiler_params=SMALL,
        name="join",
    )(kv, *came, bias)
    x_line = (move(x, far_x), move(y, across_y), x)
    y_line = (move(y, far_y), move(x, partner), y)

    heads = width // HD
    work = heads * side * 3 * side
    half = shape((side, width), bf)

    def attend(turn, line, *more):
        return pl.pallas_call(
            functools.partial(attend_kernel, turn),
            in_specs=[VMEM] * (5 + len(more)),
            out_specs=[VMEM] * 5,
            scratch_shapes=[pltpu.VMEM((HD, 3 * side), bf)] * 2
            + [pltpu.VMEM((HD, 3 * side), jnp.float32)] * 2,
            out_shape=[
                half,
                shape((heads, side, 3 * side), bf),
                block,
                block,
                shape((2, side, HD), jnp.float32),
            ],
            compiler_params=pltpu.CompilerParams(vmem_limit_bytes=32 * 2**20),
            cost_estimate=pl.CostEstimate(
                flops=10 * work * HD, bytes_accessed=6 * side * width, transcendentals=work
            ),
            name="attend",
        )(qg, *line, bias, *more)

    attn_x, ds_x, for_far_x, for_partner, own_x = attend(0, x_line)
    more = move(for_partner, partner, back=True)
    from_far_x = move(for_far_x, far_x, back=True)
    attn_y, ds_y, for_far_y, for_partner, own_y = attend(1, y_line, more)
    terms = (
        (own_x, from_far_x, move(for_partner, partner, back=True)),
        (own_y, move(for_far_y, far_y, back=True)),
    )
    dq_x, dq_y = pl.pallas_call(
        query_kernel,
        out_shape=[half, half],
        in_specs=[VMEM] * 8,
        out_specs=[VMEM] * 2,
        compiler_params=pltpu.CompilerParams(vmem_limit_bytes=16 * 2**20),
        cost_estimate=pl.CostEstimate(
            flops=4 * work * HD, bytes_accessed=4 * work, transcendentals=0
        ),
        name="query",
    )(ds_x, *x_line, ds_y, *y_line)

    pieces = pl.pallas_call(
        functools.partial(total_kernel, groups),
        out_shape=[piece] * groups,
        in_specs=[VMEM] * 5,
        out_specs=[VMEM] * groups,
        compiler_params=SMALL,
        name="total",
    )(*terms[0], *terms[1])
    returned = [pieces[0]] + [around(block, step) for step, block in enumerate(pieces[1:], 1)]
    attn_out, q_grad, filled = pl.pallas_call(
        fill_kernel,
        out_shape=[shape(queries.shape, bf)] * 2 + [shape((8, HD), jnp.float32)],
        in_specs=[VMEM] * 4 + [ANY],
        out_specs=[HBM, HBM, VMEM],
        scratch_shapes=[pltpu.SemaphoreType.DMA((4,))],
        compiler_params=SMALL,
        cost_estimate=pl.CostEstimate(
            flops=0, bytes_accessed=16 * side * width, transcendentals=0
        ),
        name="fill",
    )(attn_x, attn_y, dq_x, dq_y, returned[1])
    k_grad, v_grad = pl.pallas_call(
        functools.partial(place_kernel, groups),
        out_shape=[shape(keys.shape, bf)] * 2,
        in_specs=[VMEM] * groups + [ANY],
        out_specs=[VMEM] * 2,
        compiler_params=SMALL,
        name="place",
    )(*returned, filled)
    return (attn_out, q_grad, k_grad, v_grad)


def solution(mesh):
    heads, tokens = P(None, "cp", None, "tp"), P(None, "cp", "tp", None)
    return jax.shard_map(
        local,
        mesh=mesh,
        in_specs=(heads, tokens, tokens, heads, P()),
        out_specs=(heads, heads, tokens, tokens),
        check_vma=False,
    )
```

```python
import functools
import math

import jax
import jax.numpy as jnp
from jax import lax
from jax.experimental import pallas as pl
from jax.experimental.pallas import tpu as pltpu
from jax.sharding import PartitionSpec as P

HD = 128
FACTOR = 1.0 / math.sqrt(HD)
LOG2E = math.log2(math.e)
OUT = -1e30
VMEM = pl.BlockSpec(memory_space=pltpu.VMEM)
HBM = pl.BlockSpec(memory_space=pltpu.HBM)
ANY = pl.BlockSpec(memory_space=pl.ANY)
SMALL = pltpu.CompilerParams(vmem_limit_bytes=4 * 2**20)


def far_x(i, contexts):
    if i % 2:
        return i - 2
    return i + 2 if i + 2 < contexts else i + 1


def across_y(i, contexts):
    if i % 2:
        return min(i + 1, contexts - 1)
    return i - 1


def far_y(i, contexts):
    if i % 2:
        return i + 2 if i + 2 < contexts else i - 1
    return i - 2


def partner(i, contexts):
    return i ^ 1


def move(block, target, back=False):
    contexts = lax.axis_size("cp")
    route = [(i, target(i, contexts)) for i in range(contexts) if target(i, contexts) >= 0]
    if back:
        route = [(there, here) for here, there in route]
    return lax.ppermute(block, "cp", route)


def offset(step, core, groups):
    return jnp.where(core == 0, step, groups - step)


def around(block, step):
    contexts, groups = lax.axis_size("cp"), lax.axis_size("tp")
    route = []
    for i in range(contexts):
        turn = step if i % 2 == 0 else groups - step
        route += [(i * groups + t, i * groups + (t + turn) % groups) for t in range(groups)]
    return lax.ppermute(block, ("cp", "tp"), route)


def exchange(double, single):
    came, before = around(double, 1), around(single, 3)
    return came, around(came[1], 1), before


def dot(a, b, contract):
    return lax.dot_general(a, b, (contract, ((), ())), preferred_element_type=jnp.float32)


def aligned(index, size):
    return pl.ds(pl.multiple_of(index * size, size), size)


def views(double_ref, *singles):
    if len(singles) == 1:
        return double_ref.at[0], double_ref.at[1], singles[0]
    return double_ref.at[0], *singles


def split_kernel(groups, kv_ref, *refs):
    tp, core = lax.axis_index("tp"), lax.rem(lax.axis_index("cp"), 2)
    for step, piece in enumerate(views(*refs), 1):
        lanes = aligned(lax.rem(tp + offset(step, core, groups), groups), HD)
        for kind in range(2):
            for block, half in enumerate((core, 1 - core)):
                piece[block, kind] = kv_ref[kind, half, 0, :, lanes]


def join_kernel(groups, kv_ref, *refs):
    pieces, outs = views(*refs[:-3]), refs[-2:]
    tp, core = lax.axis_index("tp"), lax.rem(lax.axis_index("cp"), 2)
    rows = kv_ref.shape[3]
    for kind in range(2):
        for half, out in zip((core, 1 - core), outs):
            out[kind, aligned(tp, rows), :] = kv_ref[kind, half, 0, :, aligned(tp, HD)]
    for step, piece in enumerate(pieces, 1):
        source = lax.rem(tp - offset(step, core, groups) + groups, groups)
        for block, out in enumerate(outs):
            out[:, aligned(source, rows), :] = piece[block]


def total_kernel(groups, *refs):
    terms, pieces = (refs[:3], refs[3:5]), (refs[5], *views(*refs[6:]))
    tp, core = lax.axis_index("tp"), lax.rem(lax.axis_index("cp"), 2)
    rows = pieces[0].shape[2]
    for step, piece in enumerate(pieces):
        place = aligned(lax.rem(tp + offset(step, core, groups), groups), rows)
        for block in range(2):
            own, *came = [ref[:, place, :] for ref in terms[block]]
            for term in came:
                own = own + term.astype(jnp.float32)
            piece[block] = own.astype(piece.dtype)


def place_kernel(groups, *refs):
    pieces, outs = (refs[0], *views(*refs[1:-3])), refs[-2:]
    tp, core = lax.axis_index("tp"), lax.rem(lax.axis_index("cp"), 2)
    for step, piece in enumerate(pieces):
        lanes = aligned(lax.rem(tp - offset(step, core, groups) + groups, groups), HD)
        for block, half in enumerate((core, 1 - core)):
            for kind, out in enumerate(outs):
                out[half, 0, :, lanes] = piece[block, kind]


def prepare_kernel(contexts, q_ref, g_ref, len_ref, qg_ref, bias_ref, sems):
    cp = lax.axis_index("cp")
    core = lax.rem(cp, 2)
    copies = []
    for kind, ref in enumerate((q_ref, g_ref)):
        for turn, half in enumerate((core, 1 - core)):
            copies.append(
                pltpu.make_async_copy(
                    ref.at[half, 0], qg_ref.at[kind, turn], sems.at[2 * kind + turn]
                )
            )
    for copy in copies:
        copy.start()

    bf = jnp.bfloat16
    side, docs = bias_ref.shape[1], len_ref.shape[1]
    up, back = cp, 2 * contexts - 1 - cp
    blocks = (jnp.where(core == 0, up, back), jnp.where(core == 0, back, up))
    lengths = jnp.broadcast_to(len_ref[...], (8, docs))
    before = lax.broadcasted_iota(jnp.int32, (docs, docs), 0)
    after = lax.broadcasted_iota(jnp.int32, (docs, docs), 1)
    upto = (before <= after).astype(jnp.float32).astype(bf)
    coarse = (lengths // 16).astype(jnp.float32).astype(bf)
    fine = (lengths % 16).astype(jnp.float32).astype(bf)
    over = ((1,), (0,))
    ends = (16.0 * dot(coarse, upto, over) + dot(fine, upto, over))[0:1, :]
    row = lax.broadcasted_iota(jnp.int32, (side, side), 0)
    column = lax.broadcasted_iota(jnp.int32, (side, side), 1)
    key = column.astype(jnp.float32)
    shared = jnp.where(column <= row, key, key - 2.0 * side)
    for turn, block in enumerate(blocks):
        first = block * side
        position = lax.broadcasted_iota(jnp.int32, (side, docs), 0) + first
        begins = jnp.where(ends <= position.astype(jnp.float32), ends, 0.0)
        begins = jnp.max(begins, axis=1, keepdims=True) - first.astype(jnp.float32)
        bias_ref[turn, :, :side] = jnp.where(shared >= begins, 0.0, OUT)
        bias_ref[turn, :, side:] = jnp.where(key - side >= begins, 0.0, OUT)

    for copy in copies:
        copy.wait()


def fill_kernel(*refs):
    parts, (after_ref, attn_ref, dq_ref, done_ref, sems) = refs[:4], refs[4:]
    core = lax.rem(lax.axis_index("cp"), 2)
    copies = []
    for kind, ref in enumerate((attn_ref, dq_ref)):
        for turn, half in enumerate((core, 1 - core)):
            n = 2 * kind + turn
            copies.append(pltpu.make_async_copy(parts[n], ref.at[half, 0], sems.at[n]))
    for copy in copies:
        copy.start()
    done_ref[...] = jnp.zeros_like(done_ref)
    for copy in copies:
        copy.wait()


def blend(field, side):
    low = side // 2
    row = lax.broadcasted_iota(jnp.int32, (low, low), 0)
    column = lax.broadcasted_iota(jnp.int32, (low, low), 1)
    causal = column <= row
    old, own = field[:, :side], field[:, 2 * side :]
    top = jnp.concatenate(
        [jnp.where(causal, own[:low, :low], old[:low, :low]), old[:low, low:]], axis=1
    )
    bottom = jnp.concatenate(
        [own[low:, :low], jnp.where(causal, own[low:, low:], old[low:, low:])], axis=1
    )
    shared = jnp.concatenate([top, bottom], axis=0)
    return jnp.concatenate([shared, field[:, side : 2 * side]], axis=1)


def unblend(field, side):
    low = side // 2
    row = lax.broadcasted_iota(jnp.int32, (low, low), 0)
    column = lax.broadcasted_iota(jnp.int32, (low, low), 1)
    causal = column <= row
    bf = jnp.bfloat16
    none = jnp.zeros((low, low), bf)
    a, d = field[:low, :low], field[low:, low : 2 * low]
    b, c = field[:low, low : 2 * low].astype(bf), field[low:, :low].astype(bf)
    a_own, a_old = jnp.where(causal, a, 0.0).astype(bf), jnp.where(causal, 0.0, a).astype(bf)
    d_own, d_old = jnp.where(causal, d, 0.0).astype(bf), jnp.where(causal, 0.0, d).astype(bf)
    old = jnp.concatenate(
        [jnp.concatenate([a_old, b], axis=1), jnp.concatenate([none, d_old], axis=1)], axis=0
    )
    own = jnp.concatenate(
        [jnp.concatenate([a_own, none], axis=1), jnp.concatenate([c, d_own], axis=1)], axis=0
    )
    return jnp.concatenate([old, field[:, side:].astype(bf), own], axis=1)


def window(kind, *line):
    return jnp.concatenate([ref[kind] for ref in line], axis=0)


def attend_kernel(turn, qg_ref, oldest_ref, middle_ref, here_ref, bias_ref, *refs):
    if turn == 0:
        more_ref = None
    else:
        more_ref, *refs = refs
    attn_ref, ds_ref, to_oldest_ref, to_middle_ref, own_ref, kt_ref, vt_ref, dk_ref, dv_ref = refs
    side, heads = attn_ref.shape[0], ds_ref.shape[0]
    bf = jnp.bfloat16
    over, down = ((1,), (0,)), ((0,), (0,))
    keys, values = [window(kind, oldest_ref, middle_ref, here_ref) for kind in range(2)]
    kt_ref[...] = keys.T
    vt_ref[...] = values.T

    def lanes(head):
        return slice(head * HD, (head + 1) * HD)

    def products(head):
        q, g = qg_ref[0, turn, :, lanes(head)], qg_ref[1, turn, :, lanes(head)]
        return q, g, dot(q, kt_ref[...], over), dot(g, vt_ref[...], over)

    def softmax(scores):
        scaled = blend(scores, side) * (FACTOR * LOG2E) + bias_ref[turn]
        raised = jnp.exp2(scaled - jnp.max(scaled, axis=1, keepdims=True))
        return raised * (1.0 / jnp.sum(raised, axis=1, keepdims=True))

    def finish(head, q, g, probs_low, ds):
        ds_ref[head] = ds
        value_term, key_term = dot(g, probs_low, down), dot(q, ds, down)
        if head == 0:
            dv_ref[...], dk_ref[...] = value_term, key_term
        else:
            dv_ref[...] += value_term
            dk_ref[...] += key_term

    pending = None
    ahead = products(0)
    for head in range(heads):
        q, g, scores, dprobs = ahead
        if head + 1 < heads:
            ahead = products(head + 1)
        probs = softmax(scores)
        probs_low = unblend(probs, side)
        attn = dot(probs_low, values, over).astype(bf)
        attn_ref[:, lanes(head)] = attn
        if pending is not None:
            finish(*pending)
        delta = jnp.sum(attn.astype(jnp.float32) * g.astype(jnp.float32), axis=1, keepdims=True)
        ds = unblend(probs * (blend(dprobs, side) - delta), side)
        pending = (head, q, g, probs_low, ds)
    finish(*pending)
    for kind, (ref, factor) in enumerate(((dk_ref, FACTOR), (dv_ref, 1.0))):
        for n, out in enumerate((to_oldest_ref, to_middle_ref, own_ref)):
            term = ref[:, n * side : (n + 1) * side].T * factor
            if n == 0 and more_ref is not None:
                term = term + more_ref[kind].astype(jnp.float32)
            out[kind] = term.astype(out.dtype)


def query_kernel(*refs):
    inputs, outs = refs[:-2], refs[-2:]
    for turn, out in enumerate(outs):
        ds_ref, *line = inputs[4 * turn : 4 * turn + 4]
        heads = ds_ref.shape[0]
        keys = window(0, *line)
        for head in range(heads):
            dq = dot(ds_ref[head], keys, ((1,), (0,))) * FACTOR
            out[:, head * HD : (head + 1) * HD] = dq.astype(out.dtype)


def local(queries, keys, values, out_grad, doc_lengths):
    side, width = queries.shape[2], queries.shape[3]
    contexts, groups = lax.axis_size("cp"), lax.axis_size("tp")
    rows = keys.shape[2]
    bf = jnp.bfloat16
    shape = jax.ShapeDtypeStruct
    piece, double = shape((2, 2, rows, HD), bf), shape((2, 2, 2, rows, HD), bf)

    kv = jnp.stack([keys, values])
    sent = pl.pallas_call(
        functools.partial(split_kernel, groups),
        out_shape=[double, piece],
        in_specs=[VMEM],
        out_specs=[VMEM] * 2,
        compiler_params=SMALL,
        name="split",
    )(kv)
    came = exchange(*sent)
    qg, bias = pl.pallas_call(
        functools.partial(prepare_kernel, contexts),
        out_shape=[shape((2, 2, side, width), bf), shape((2, side, 2 * side), jnp.float32)],
        in_specs=[HBM, HBM, VMEM],
        out_specs=[VMEM] * 2,
        scratch_shapes=[pltpu.SemaphoreType.DMA((4,))],
        compiler_params=SMALL,
        cost_estimate=pl.CostEstimate(
            flops=0, bytes_accessed=16 * side * width, transcendentals=0
        ),
        name="prepare",
    )(queries, out_grad, doc_lengths[None, :])
    block = shape((2, side, HD), bf)
    x, y = pl.pallas_call(
        functools.partial(join_kernel, groups),
        out_shape=[block] * 2,
        in_specs=[VMEM] * groups + [ANY],
        out_specs=[VMEM] * 2,
        compiler_params=SMALL,
        name="join",
    )(kv, *came, bias)
    x_line = (move(x, far_x), move(y, across_y), x)
    y_line = (move(y, far_y), move(x, partner), y)

    heads = width // HD
    work = heads * side * 3 * side
    half = shape((side, width), bf)

    def attend(turn, line, *more):
        return pl.pallas_call(
            functools.partial(attend_kernel, turn),
            in_specs=[VMEM] * (5 + len(more)),
            out_specs=[VMEM] * 5,
            scratch_shapes=[pltpu.VMEM((HD, 3 * side), bf)] * 2
            + [pltpu.VMEM((HD, 3 * side), jnp.float32)] * 2,
            out_shape=[
                half,
                shape((heads, side, 3 * side), bf),
                block,
                block,
                shape((2, side, HD), jnp.float32),
            ],
            compiler_params=pltpu.CompilerParams(vmem_limit_bytes=32 * 2**20),
            cost_estimate=pl.CostEstimate(
                flops=10 * work * HD, bytes_accessed=6 * side * width, transcendentals=work
            ),
            name="attend",
        )(qg, *line, bias, *more)

    attn_x, ds_x, for_far_x, for_partner, own_x = attend(0, x_line)
    more = move(for_partner, partner, back=True)
    from_far_x = move(for_far_x, far_x, back=True)
    attn_y, ds_y, for_far_y, for_partner, own_y = attend(1, y_line, more)
    terms = (
        (own_x, from_far_x, move(for_partner, partner, back=True)),
        (own_y, move(for_far_y, far_y, back=True)),
    )
    dq_x, dq_y = pl.pallas_call(
        query_kernel,
        out_shape=[half, half],
        in_specs=[VMEM] * 8,
        out_specs=[VMEM] * 2,
        compiler_params=pltpu.CompilerParams(vmem_limit_bytes=16 * 2**20),
        cost_estimate=pl.CostEstimate(
            flops=4 * work * HD, bytes_accessed=4 * work, transcendentals=0
        ),
        name="query",
    )(ds_x, *x_line, ds_y, *y_line)

    kept, *sent = pl.pallas_call(
        functools.partial(total_kernel, groups),
        out_shape=[piece, double, piece],
        in_specs=[VMEM] * 5,
        out_specs=[VMEM] * 3,
        compiler_params=SMALL,
        name="total",
    )(*terms[0], *terms[1])
    returned = exchange(*sent)
    attn_out, q_grad, filled = pl.pallas_call(
        fill_kernel,
        out_shape=[shape(queries.shape, bf)] * 2 + [shape((8, HD), jnp.float32)],
        in_specs=[VMEM] * 4 + [ANY],
        out_specs=[HBM, HBM, VMEM],
        scratch_shapes=[pltpu.SemaphoreType.DMA((4,))],
        compiler_params=SMALL,
        cost_estimate=pl.CostEstimate(
            flops=0, bytes_accessed=16 * side * width, transcendentals=0
        ),
        name="fill",
    )(attn_x, attn_y, dq_x, dq_y, returned[2])
    k_grad, v_grad = pl.pallas_call(
        functools.partial(place_kernel, groups),
        out_shape=[shape(keys.shape, bf)] * 2,
        in_specs=[VMEM] * groups + [ANY],
        out_specs=[VMEM] * 2,
        compiler_params=SMALL,
        name="place",
    )(kept, *returned, filled)
    return (attn_out, q_grad, k_grad, v_grad)


def solution(mesh):
    heads, tokens = P(None, "cp", None, "tp"), P(None, "cp", "tp", None)
    return jax.shard_map(
        local,
        mesh=mesh,
        in_specs=(heads, tokens, tokens, heads, P()),
        out_specs=(heads, heads, tokens, tokens),
        check_vma=False,
    )
```

```python
import functools
import math

import jax
import jax.numpy as jnp
from jax import lax
from jax.experimental import pallas as pl
from jax.experimental.pallas import tpu as pltpu
from jax.sharding import PartitionSpec as P

HD = 128
FACTOR = 1.0 / math.sqrt(HD)
LOG2E = math.log2(math.e)
OUT = -1e30
VMEM = pl.BlockSpec(memory_space=pltpu.VMEM)
HBM = pl.BlockSpec(memory_space=pltpu.HBM)
ANY = pl.BlockSpec(memory_space=pl.ANY)
SMALL = pltpu.CompilerParams(vmem_limit_bytes=4 * 2**20)


def far_x(i, contexts):
    if i % 2:
        return i - 2
    return i + 2 if i + 2 < contexts else i + 1


def across_y(i, contexts):
    if i % 2:
        return min(i + 1, contexts - 1)
    return i - 1


def far_y(i, contexts):
    if i % 2:
        return i + 2 if i + 2 < contexts else i - 1
    return i - 2


def partner(i, contexts):
    return i ^ 1


def move(block, target, back=False):
    contexts = lax.axis_size("cp")
    route = [(i, target(i, contexts)) for i in range(contexts) if target(i, contexts) >= 0]
    if back:
        route = [(there, here) for here, there in route]
    return lax.ppermute(block, "cp", route)


def apart(step, core):
    return step if step == 2 else jnp.where(core == 0, step, 4 - step)


def swap(block, step):
    contexts, groups = lax.axis_size("cp"), lax.axis_size("tp")
    route = []
    for i in range(contexts):
        bits = step if i % 2 == 0 else 4 - step
        route += [(i * groups + t, i * groups + (t ^ bits)) for t in range(groups)]
    return lax.ppermute(block, ("cp", "tp"), route)


def exchange(double, single):
    first = swap(double, 1)
    return first, swap(jnp.stack([single, first[1]]), 3)


def dot(a, b, contract):
    return lax.dot_general(a, b, (contract, ((), ())), preferred_element_type=jnp.float32)


def aligned(index, size):
    return pl.ds(pl.multiple_of(index * size, size), size)


def leaving(double_ref, single_ref):
    return double_ref.at[0], double_ref.at[1], single_ref


def arriving(first_ref, second_ref):
    return first_ref.at[0], second_ref.at[1], second_ref.at[0]


def split_kernel(kv_ref, *refs):
    tp, core = lax.axis_index("tp"), lax.rem(lax.axis_index("cp"), 2)
    for step, piece in enumerate(leaving(*refs), 1):
        lanes = aligned(tp ^ apart(step, core), HD)
        for kind in range(2):
            for block, half in enumerate((core, 1 - core)):
                piece[block, kind] = kv_ref[kind, half, 0, :, lanes]


def join_kernel(kv_ref, *refs):
    pieces, outs = arriving(*refs[:-3]), refs[-2:]
    tp, core = lax.axis_index("tp"), lax.rem(lax.axis_index("cp"), 2)
    rows = kv_ref.shape[3]
    for kind in range(2):
        for half, out in zip((core, 1 - core), outs):
            out[kind, aligned(tp, rows), :] = kv_ref[kind, half, 0, :, aligned(tp, HD)]
    for step, piece in enumerate(pieces, 1):
        source = tp ^ apart(step, core)
        for block, out in enumerate(outs):
            out[:, aligned(source, rows), :] = piece[block]


def total_kernel(*refs):
    terms, pieces = (refs[:3], refs[3:5]), (refs[5], *leaving(*refs[6:]))
    tp, core = lax.axis_index("tp"), lax.rem(lax.axis_index("cp"), 2)
    rows = pieces[0].shape[2]
    for step, piece in enumerate(pieces):
        place = aligned(tp if step == 0 else tp ^ apart(step, core), rows)
        for block in range(2):
            own, *came = [ref[:, place, :] for ref in terms[block]]
            for term in came:
                own = own + term.astype(jnp.float32)
            piece[block] = own.astype(piece.dtype)


def place_kernel(*refs):
    pieces, outs = (refs[0], *arriving(*refs[1:-3])), refs[-2:]
    tp, core = lax.axis_index("tp"), lax.rem(lax.axis_index("cp"), 2)
    for step, piece in enumerate(pieces):
        lanes = aligned(tp if step == 0 else tp ^ apart(step, core), HD)
        for block, half in enumerate((core, 1 - core)):
            for kind, out in enumerate(outs):
                out[half, 0, :, lanes] = piece[block, kind]


def prepare_kernel(contexts, q_ref, g_ref, len_ref, qg_ref, bias_ref, sems):
    cp = lax.axis_index("cp")
    core = lax.rem(cp, 2)
    copies = []
    for kind, ref in enumerate((q_ref, g_ref)):
        for turn, half in enumerate((core, 1 - core)):
            copies.append(
                pltpu.make_async_copy(
                    ref.at[half, 0], qg_ref.at[kind, turn], sems.at[2 * kind + turn]
                )
            )
    for copy in copies:
        copy.start()

    bf = jnp.bfloat16
    side, docs = bias_ref.shape[1], len_ref.shape[1]
    up, back = cp, 2 * contexts - 1 - cp
    blocks = (jnp.where(core == 0, up, back), jnp.where(core == 0, back, up))
    lengths = jnp.broadcast_to(len_ref[...], (8, docs))
    before = lax.broadcasted_iota(jnp.int32, (docs, docs), 0)
    after = lax.broadcasted_iota(jnp.int32, (docs, docs), 1)
    upto = (before <= after).astype(jnp.float32).astype(bf)
    coarse = (lengths // 16).astype(jnp.float32).astype(bf)
    fine = (lengths % 16).astype(jnp.float32).astype(bf)
    over = ((1,), (0,))
    ends = (16.0 * dot(coarse, upto, over) + dot(fine, upto, over))[0:1, :]
    row = lax.broadcasted_iota(jnp.int32, (side, side), 0)
    column = lax.broadcasted_iota(jnp.int32, (side, side), 1)
    key = column.astype(jnp.float32)
    shared = jnp.where(column <= row, key, key - 2.0 * side)
    for turn, block in enumerate(blocks):
        first = block * side
        position = lax.broadcasted_iota(jnp.int32, (side, docs), 0) + first
        begins = jnp.where(ends <= position.astype(jnp.float32), ends, 0.0)
        begins = jnp.max(begins, axis=1, keepdims=True) - first.astype(jnp.float32)
        bias_ref[turn, :, :side] = jnp.where(shared >= begins, 0.0, OUT)
        bias_ref[turn, :, side:] = jnp.where(key - side >= begins, 0.0, OUT)

    for copy in copies:
        copy.wait()


def fill_kernel(*refs):
    parts, (after_ref, attn_ref, dq_ref, done_ref, sems) = refs[:4], refs[4:]
    core = lax.rem(lax.axis_index("cp"), 2)
    copies = []
    for kind, ref in enumerate((attn_ref, dq_ref)):
        for turn, half in enumerate((core, 1 - core)):
            n = 2 * kind + turn
            copies.append(pltpu.make_async_copy(parts[n], ref.at[half, 0], sems.at[n]))
    for copy in copies:
        copy.start()
    done_ref[...] = jnp.zeros_like(done_ref)
    for copy in copies:
        copy.wait()


def blend(field, side):
    low = side // 2
    row = lax.broadcasted_iota(jnp.int32, (low, low), 0)
    column = lax.broadcasted_iota(jnp.int32, (low, low), 1)
    causal = column <= row
    old, own = field[:, :side], field[:, 2 * side :]
    top = jnp.concatenate(
        [jnp.where(causal, own[:low, :low], old[:low, :low]), old[:low, low:]], axis=1
    )
    bottom = jnp.concatenate(
        [own[low:, :low], jnp.where(causal, own[low:, low:], old[low:, low:])], axis=1
    )
    shared = jnp.concatenate([top, bottom], axis=0)
    return jnp.concatenate([shared, field[:, side : 2 * side]], axis=1)


def unblend(field, side):
    low = side // 2
    row = lax.broadcasted_iota(jnp.int32, (low, low), 0)
    column = lax.broadcasted_iota(jnp.int32, (low, low), 1)
    causal = column <= row
    bf = jnp.bfloat16
    none = jnp.zeros((low, low), bf)
    a, d = field[:low, :low], field[low:, low : 2 * low]
    b, c = field[:low, low : 2 * low].astype(bf), field[low:, :low].astype(bf)
    a_own, a_old = jnp.where(causal, a, 0.0).astype(bf), jnp.where(causal, 0.0, a).astype(bf)
    d_own, d_old = jnp.where(causal, d, 0.0).astype(bf), jnp.where(causal, 0.0, d).astype(bf)
    old = jnp.concatenate(
        [jnp.concatenate([a_old, b], axis=1), jnp.concatenate([none, d_old], axis=1)], axis=0
    )
    own = jnp.concatenate(
        [jnp.concatenate([a_own, none], axis=1), jnp.concatenate([c, d_own], axis=1)], axis=0
    )
    return jnp.concatenate([old, field[:, side:].astype(bf), own], axis=1)


def window(kind, *line):
    return jnp.concatenate([ref[kind] for ref in line], axis=0)


def attend_kernel(turn, qg_ref, oldest_ref, middle_ref, here_ref, bias_ref, *refs):
    if turn == 0:
        more_ref = None
    else:
        more_ref, *refs = refs
    attn_ref, ds_ref, to_oldest_ref, to_middle_ref, own_ref, kt_ref, vt_ref, dk_ref, dv_ref = refs
    side, heads = attn_ref.shape[0], ds_ref.shape[0]
    bf = jnp.bfloat16
    over, down = ((1,), (0,)), ((0,), (0,))
    keys, values = [window(kind, oldest_ref, middle_ref, here_ref) for kind in range(2)]
    kt_ref[...] = keys.T
    vt_ref[...] = values.T

    def lanes(head):
        return slice(head * HD, (head + 1) * HD)

    def products(head):
        q, g = qg_ref[0, turn, :, lanes(head)], qg_ref[1, turn, :, lanes(head)]
        return q, g, dot(q, kt_ref[...], over), dot(g, vt_ref[...], over)

    def softmax(scores):
        scaled = blend(scores, side) * (FACTOR * LOG2E) + bias_ref[turn]
        raised = jnp.exp2(scaled - jnp.max(scaled, axis=1, keepdims=True))
        return raised * (1.0 / jnp.sum(raised, axis=1, keepdims=True))

    def finish(head, q, g, probs_low, ds):
        ds_ref[head] = ds
        value_term, key_term = dot(g, probs_low, down), dot(q, ds, down)
        if head == 0:
            dv_ref[...], dk_ref[...] = value_term, key_term
        else:
            dv_ref[...] += value_term
            dk_ref[...] += key_term

    pending = None
    ahead = products(0)
    for head in range(heads):
        q, g, scores, dprobs = ahead
        if head + 1 < heads:
            ahead = products(head + 1)
        probs = softmax(scores)
        probs_low = unblend(probs, side)
        attn = dot(probs_low, values, over).astype(bf)
        attn_ref[:, lanes(head)] = attn
        if pending is not None:
            finish(*pending)
        delta = jnp.sum(attn.astype(jnp.float32) * g.astype(jnp.float32), axis=1, keepdims=True)
        ds = unblend(probs * (blend(dprobs, side) - delta), side)
        pending = (head, q, g, probs_low, ds)
    finish(*pending)
    for kind, (ref, factor) in enumerate(((dk_ref, FACTOR), (dv_ref, 1.0))):
        for n, out in enumerate((to_oldest_ref, to_middle_ref, own_ref)):
            term = ref[:, n * side : (n + 1) * side].T * factor
            if n == 0 and more_ref is not None:
                term = term + more_ref[kind].astype(jnp.float32)
            out[kind] = term.astype(out.dtype)


def query_kernel(*refs):
    inputs, outs = refs[:-2], refs[-2:]
    for turn, out in enumerate(outs):
        ds_ref, *line = inputs[4 * turn : 4 * turn + 4]
        heads = ds_ref.shape[0]
        keys = window(0, *line)
        for head in range(heads):
            dq = dot(ds_ref[head], keys, ((1,), (0,))) * FACTOR
            out[:, head * HD : (head + 1) * HD] = dq.astype(out.dtype)


def local(queries, keys, values, out_grad, doc_lengths):
    side, width = queries.shape[2], queries.shape[3]
    contexts = lax.axis_size("cp")
    rows = keys.shape[2]
    bf = jnp.bfloat16
    shape = jax.ShapeDtypeStruct
    piece, double = shape((2, 2, rows, HD), bf), shape((2, 2, 2, rows, HD), bf)

    kv = jnp.stack([keys, values])
    sent = pl.pallas_call(
        split_kernel,
        out_shape=[double, piece],
        in_specs=[VMEM],
        out_specs=[VMEM] * 2,
        compiler_params=SMALL,
        name="split",
    )(kv)
    came = exchange(*sent)
    qg, bias = pl.pallas_call(
        functools.partial(prepare_kernel, contexts),
        out_shape=[shape((2, 2, side, width), bf), shape((2, side, 2 * side), jnp.float32)],
        in_specs=[HBM, HBM, VMEM],
        out_specs=[VMEM] * 2,
        scratch_shapes=[pltpu.SemaphoreType.DMA((4,))],
        compiler_params=SMALL,
        cost_estimate=pl.CostEstimate(
            flops=0, bytes_accessed=16 * side * width, transcendentals=0
        ),
        name="prepare",
    )(queries, out_grad, doc_lengths[None, :])
    block = shape((2, side, HD), bf)
    x, y = pl.pallas_call(
        join_kernel,
        out_shape=[block] * 2,
        in_specs=[VMEM] * 3 + [ANY],
        out_specs=[VMEM] * 2,
        compiler_params=SMALL,
        name="join",
    )(kv, *came, bias)
    x_line = (move(x, far_x), move(y, across_y), x)
    y_line = (move(y, far_y), move(x, partner), y)

    heads = width // HD
    work = heads * side * 3 * side
    half = shape((side, width), bf)

    def attend(turn, line, *more):
        return pl.pallas_call(
            functools.partial(attend_kernel, turn),
            in_specs=[VMEM] * (5 + len(more)),
            out_specs=[VMEM] * 5,
            scratch_shapes=[pltpu.VMEM((HD, 3 * side), bf)] * 2
            + [pltpu.VMEM((HD, 3 * side), jnp.float32)] * 2,
            out_shape=[
                half,
                shape((heads, side, 3 * side), bf),
                block,
                block,
                shape((2, side, HD), jnp.float32),
            ],
            compiler_params=pltpu.CompilerParams(vmem_limit_bytes=32 * 2**20),
            cost_estimate=pl.CostEstimate(
                flops=10 * work * HD, bytes_accessed=6 * side * width, transcendentals=work
            ),
            name="attend",
        )(qg, *line, bias, *more)

    attn_x, ds_x, for_far_x, for_partner, own_x = attend(0, x_line)
    more = move(for_partner, partner, back=True)
    from_far_x = move(for_far_x, far_x, back=True)
    attn_y, ds_y, for_far_y, for_partner, own_y = attend(1, y_line, more)
    terms = (
        (own_x, from_far_x, move(for_partner, partner, back=True)),
        (own_y, move(for_far_y, far_y, back=True)),
    )
    dq_x, dq_y = pl.pallas_call(
        query_kernel,
        out_shape=[half, half],
        in_specs=[VMEM] * 8,
        out_specs=[VMEM] * 2,
        compiler_params=pltpu.CompilerParams(vmem_limit_bytes=16 * 2**20),
        cost_estimate=pl.CostEstimate(
            flops=4 * work * HD, bytes_accessed=4 * work, transcendentals=0
        ),
        name="query",
    )(ds_x, *x_line, ds_y, *y_line)

    kept, *sent = pl.pallas_call(
        total_kernel,
        out_shape=[piece, double, piece],
        in_specs=[VMEM] * 5,
        out_specs=[VMEM] * 3,
        compiler_params=SMALL,
        name="total",
    )(*terms[0], *terms[1])
    returned = exchange(*sent)
    attn_out, q_grad, filled = pl.pallas_call(
        fill_kernel,
        out_shape=[shape(queries.shape, bf)] * 2 + [shape((8, HD), jnp.float32)],
        in_specs=[VMEM] * 4 + [ANY],
        out_specs=[HBM, HBM, VMEM],
        scratch_shapes=[pltpu.SemaphoreType.DMA((4,))],
        compiler_params=SMALL,
        cost_estimate=pl.CostEstimate(
            flops=0, bytes_accessed=16 * side * width, transcendentals=0
        ),
        name="fill",
    )(attn_x, attn_y, dq_x, dq_y, returned[0])
    k_grad, v_grad = pl.pallas_call(
        place_kernel,
        out_shape=[shape(keys.shape, bf)] * 2,
        in_specs=[VMEM] * 3 + [ANY],
        out_specs=[VMEM] * 2,
        compiler_params=SMALL,
        name="place",
    )(kept, *returned, filled)
    return (attn_out, q_grad, k_grad, v_grad)


def solution(mesh):
    heads, tokens = P(None, "cp", None, "tp"), P(None, "cp", "tp", None)
    return jax.shard_map(
        local,
        mesh=mesh,
        in_specs=(heads, tokens, tokens, heads, P()),
        out_specs=(heads, heads, tokens, tokens),
        check_vma=False,
    )
```

```python
import functools
import math

import jax
import jax.numpy as jnp
from jax import lax
from jax.experimental import pallas as pl
from jax.experimental.pallas import tpu as pltpu
from jax.sharding import PartitionSpec as P

HD = 128
FACTOR = 1.0 / math.sqrt(HD)
LOG2E = math.log2(math.e)
OUT = -1e30
VMEM = pl.BlockSpec(memory_space=pltpu.VMEM)
HBM = pl.BlockSpec(memory_space=pltpu.HBM)
ANY = pl.BlockSpec(memory_space=pl.ANY)
SMALL = pltpu.CompilerParams(vmem_limit_bytes=4 * 2**20)


def far_x(i, contexts):
    if i % 2:
        return i - 2
    return i + 2 if i + 2 < contexts else i + 1


def across_y(i, contexts):
    if i % 2:
        return min(i + 1, contexts - 1)
    return i - 1


def far_y(i, contexts):
    if i % 2:
        return i + 2 if i + 2 < contexts else i - 1
    return i - 2


def partner(i, contexts):
    return i ^ 1


def move(block, target, back=False):
    contexts = lax.axis_size("cp")
    route = [(i, target(i, contexts)) for i in range(contexts) if target(i, contexts) >= 0]
    if back:
        route = [(there, here) for here, there in route]
    return lax.ppermute(block, "cp", route)


def offset(step, core, groups):
    return jnp.where(core == 0, step, groups - step)


def around(block, step):
    contexts, groups = lax.axis_size("cp"), lax.axis_size("tp")
    route = []
    for i in range(contexts):
        turn = step if i % 2 == 0 else groups - step
        route += [(i * groups + t, i * groups + (t + turn) % groups) for t in range(groups)]
    return lax.ppermute(block, ("cp", "tp"), route)


ARRIVAL = (2, 1, 3)


def exchange(pieces):
    return [around(pieces[step - 1], step) for step in ARRIVAL]


def dot(a, b, contract):
    return lax.dot_general(a, b, (contract, ((), ())), preferred_element_type=jnp.float32)


def aligned(index, size):
    return pl.ds(pl.multiple_of(index * size, size), size)


def split_kernel(groups, kv_ref, *pieces):
    tp, core = lax.axis_index("tp"), lax.rem(lax.axis_index("cp"), 2)
    for step, piece in enumerate(pieces, 1):
        lanes = aligned(lax.rem(tp + offset(step, core, groups), groups), HD)
        for kind in range(2):
            for block, half in enumerate((core, 1 - core)):
                piece[block, kind] = kv_ref[kind, half, 0, :, lanes]


def join_kernel(groups, kv_ref, *refs):
    pieces, outs = refs[:-3], refs[-2:]
    tp, core = lax.axis_index("tp"), lax.rem(lax.axis_index("cp"), 2)
    rows = kv_ref.shape[3]
    for kind in range(2):
        for half, out in zip((core, 1 - core), outs):
            out[kind, aligned(tp, rows), :] = kv_ref[kind, half, 0, :, aligned(tp, HD)]
    for step, piece in zip(ARRIVAL, pieces):
        source = lax.rem(tp - offset(step, core, groups) + groups, groups)
        for block, out in enumerate(outs):
            out[:, aligned(source, rows), :] = piece[block]


def total_kernel(groups, *refs):
    terms, pieces = (refs[:3], refs[3:5]), refs[5:]
    tp, core = lax.axis_index("tp"), lax.rem(lax.axis_index("cp"), 2)
    rows = pieces[0].shape[2]
    for step, piece in enumerate(pieces):
        place = aligned(lax.rem(tp + offset(step, core, groups), groups), rows)
        for block in range(2):
            own, *came = [ref[:, place, :] for ref in terms[block]]
            for term in came:
                own = own + term.astype(jnp.float32)
            piece[block] = own.astype(piece.dtype)


def place_kernel(groups, *refs):
    pieces, outs = refs[:-3], refs[-2:]
    tp, core = lax.axis_index("tp"), lax.rem(lax.axis_index("cp"), 2)
    for step, piece in zip((0, *ARRIVAL), pieces):
        lanes = aligned(lax.rem(tp - offset(step, core, groups) + groups, groups), HD)
        for block, half in enumerate((core, 1 - core)):
            for kind, out in enumerate(outs):
                out[half, 0, :, lanes] = piece[block, kind]


def prepare_kernel(contexts, q_ref, g_ref, len_ref, qg_ref, bias_ref, sems):
    cp = lax.axis_index("cp")
    core = lax.rem(cp, 2)
    copies = []
    for kind, ref in enumerate((q_ref, g_ref)):
        for turn, half in enumerate((core, 1 - core)):
            copies.append(
                pltpu.make_async_copy(
                    ref.at[half, 0], qg_ref.at[kind, turn], sems.at[2 * kind + turn]
                )
            )
    for copy in copies:
        copy.start()

    bf = jnp.bfloat16
    side, docs = bias_ref.shape[1], len_ref.shape[1]
    up, back = cp, 2 * contexts - 1 - cp
    blocks = (jnp.where(core == 0, up, back), jnp.where(core == 0, back, up))
    lengths = jnp.broadcast_to(len_ref[...], (8, docs))
    before = lax.broadcasted_iota(jnp.int32, (docs, docs), 0)
    after = lax.broadcasted_iota(jnp.int32, (docs, docs), 1)
    upto = (before <= after).astype(jnp.float32).astype(bf)
    coarse = (lengths // 16).astype(jnp.float32).astype(bf)
    fine = (lengths % 16).astype(jnp.float32).astype(bf)
    over = ((1,), (0,))
    ends = (16.0 * dot(coarse, upto, over) + dot(fine, upto, over))[0:1, :]
    row = lax.broadcasted_iota(jnp.int32, (side, side), 0)
    column = lax.broadcasted_iota(jnp.int32, (side, side), 1)
    key = column.astype(jnp.float32)
    shared = jnp.where(column <= row, key, key - 2.0 * side)
    for turn, block in enumerate(blocks):
        first = block * side
        position = lax.broadcasted_iota(jnp.int32, (side, docs), 0) + first
        begins = jnp.where(ends <= position.astype(jnp.float32), ends, 0.0)
        begins = jnp.max(begins, axis=1, keepdims=True) - first.astype(jnp.float32)
        bias_ref[turn, :, :side] = jnp.where(shared >= begins, 0.0, OUT)
        bias_ref[turn, :, side:] = jnp.where(key - side >= begins, 0.0, OUT)

    for copy in copies:
        copy.wait()


def fill_kernel(*refs):
    parts, (after_ref, attn_ref, dq_ref, done_ref, sems) = refs[:4], refs[4:]
    core = lax.rem(lax.axis_index("cp"), 2)
    copies = []
    for kind, ref in enumerate((attn_ref, dq_ref)):
        for turn, half in enumerate((core, 1 - core)):
            n = 2 * kind + turn
            copies.append(pltpu.make_async_copy(parts[n], ref.at[half, 0], sems.at[n]))
    for copy in copies:
        copy.start()
    done_ref[...] = jnp.zeros_like(done_ref)
    for copy in copies:
        copy.wait()


def blend(field, side):
    low = side // 2
    row = lax.broadcasted_iota(jnp.int32, (low, low), 0)
    column = lax.broadcasted_iota(jnp.int32, (low, low), 1)
    causal = column <= row
    old, own = field[:, :side], field[:, 2 * side :]
    top = jnp.concatenate(
        [jnp.where(causal, own[:low, :low], old[:low, :low]), old[:low, low:]], axis=1
    )
    bottom = jnp.concatenate(
        [own[low:, :low], jnp.where(causal, own[low:, low:], old[low:, low:])], axis=1
    )
    shared = jnp.concatenate([top, bottom], axis=0)
    return jnp.concatenate([shared, field[:, side : 2 * side]], axis=1)


def unblend(field, side):
    low = side // 2
    row = lax.broadcasted_iota(jnp.int32, (low, low), 0)
    column = lax.broadcasted_iota(jnp.int32, (low, low), 1)
    causal = column <= row
    bf = jnp.bfloat16
    none = jnp.zeros((low, low), bf)
    a, d = field[:low, :low], field[low:, low : 2 * low]
    b, c = field[:low, low : 2 * low].astype(bf), field[low:, :low].astype(bf)
    a_own, a_old = jnp.where(causal, a, 0.0).astype(bf), jnp.where(causal, 0.0, a).astype(bf)
    d_own, d_old = jnp.where(causal, d, 0.0).astype(bf), jnp.where(causal, 0.0, d).astype(bf)
    old = jnp.concatenate(
        [jnp.concatenate([a_old, b], axis=1), jnp.concatenate([none, d_old], axis=1)], axis=0
    )
    own = jnp.concatenate(
        [jnp.concatenate([a_own, none], axis=1), jnp.concatenate([c, d_own], axis=1)], axis=0
    )
    return jnp.concatenate([old, field[:, side:].astype(bf), own], axis=1)


def window(kind, *line):
    return jnp.concatenate([ref[kind] for ref in line], axis=0)


def attend_kernel(turn, qg_ref, oldest_ref, middle_ref, here_ref, bias_ref, *refs):
    if turn == 0:
        more_ref = None
    else:
        more_ref, *refs = refs
    attn_ref, ds_ref, to_oldest_ref, to_middle_ref, own_ref, kt_ref, vt_ref, dk_ref, dv_ref = refs
    side, heads = attn_ref.shape[0], ds_ref.shape[0]
    bf = jnp.bfloat16
    over, down = ((1,), (0,)), ((0,), (0,))
    keys, values = [window(kind, oldest_ref, middle_ref, here_ref) for kind in range(2)]
    kt_ref[...] = keys.T
    vt_ref[...] = values.T

    def lanes(head):
        return slice(head * HD, (head + 1) * HD)

    def products(head):
        q, g = qg_ref[0, turn, :, lanes(head)], qg_ref[1, turn, :, lanes(head)]
        return q, g, dot(q, kt_ref[...], over), dot(g, vt_ref[...], over)

    def softmax(scores):
        scaled = blend(scores, side) * (FACTOR * LOG2E) + bias_ref[turn]
        raised = jnp.exp2(scaled - jnp.max(scaled, axis=1, keepdims=True))
        return raised * (1.0 / jnp.sum(raised, axis=1, keepdims=True))

    def finish(head, q, g, probs_low, ds):
        ds_ref[head] = ds
        value_term, key_term = dot(g, probs_low, down), dot(q, ds, down)
        if head == 0:
            dv_ref[...], dk_ref[...] = value_term, key_term
        else:
            dv_ref[...] += value_term
            dk_ref[...] += key_term

    pending = None
    ahead = products(0)
    for head in range(heads):
        q, g, scores, dprobs = ahead
        if head + 1 < heads:
            ahead = products(head + 1)
        probs = softmax(scores)
        probs_low = unblend(probs, side)
        attn = dot(probs_low, values, over).astype(bf)
        attn_ref[:, lanes(head)] = attn
        if pending is not None:
            finish(*pending)
        delta = jnp.sum(attn.astype(jnp.float32) * g.astype(jnp.float32), axis=1, keepdims=True)
        ds = unblend(probs * (blend(dprobs, side) - delta), side)
        pending = (head, q, g, probs_low, ds)
    finish(*pending)
    for kind, (ref, factor) in enumerate(((dk_ref, FACTOR), (dv_ref, 1.0))):
        for n, out in enumerate((to_oldest_ref, to_middle_ref, own_ref)):
            term = ref[:, n * side : (n + 1) * side].T * factor
            if n == 0 and more_ref is not None:
                term = term + more_ref[kind].astype(jnp.float32)
            out[kind] = term.astype(out.dtype)


def query_kernel(*refs):
    inputs, outs = refs[:-2], refs[-2:]
    for turn, out in enumerate(outs):
        ds_ref, *line = inputs[4 * turn : 4 * turn + 4]
        heads = ds_ref.shape[0]
        keys = window(0, *line)
        for head in range(heads):
            dq = dot(ds_ref[head], keys, ((1,), (0,))) * FACTOR
            out[:, head * HD : (head + 1) * HD] = dq.astype(out.dtype)


def local(queries, keys, values, out_grad, doc_lengths):
    side, width = queries.shape[2], queries.shape[3]
    contexts, groups = lax.axis_size("cp"), lax.axis_size("tp")
    rows = keys.shape[2]
    bf = jnp.bfloat16
    shape = jax.ShapeDtypeStruct
    piece = shape((2, 2, rows, HD), bf)

    kv = jnp.stack([keys, values])
    sent = pl.pallas_call(
        functools.partial(split_kernel, groups),
        out_shape=[piece] * (groups - 1),
        in_specs=[VMEM],
        out_specs=[VMEM] * (groups - 1),
        compiler_params=SMALL,
        name="split",
    )(kv)
    came = exchange(sent)
    qg, bias = pl.pallas_call(
        functools.partial(prepare_kernel, contexts),
        out_shape=[shape((2, 2, side, width), bf), shape((2, side, 2 * side), jnp.float32)],
        in_specs=[HBM, HBM, VMEM],
        out_specs=[VMEM] * 2,
        scratch_shapes=[pltpu.SemaphoreType.DMA((4,))],
        compiler_params=SMALL,
        cost_estimate=pl.CostEstimate(
            flops=0, bytes_accessed=16 * side * width, transcendentals=0
        ),
        name="prepare",
    )(queries, out_grad, doc_lengths[None, :])
    block = shape((2, side, HD), bf)
    x, y = pl.pallas_call(
        functools.partial(join_kernel, groups),
        out_shape=[block] * 2,
        in_specs=[VMEM] * groups + [ANY],
        out_specs=[VMEM] * 2,
        compiler_params=SMALL,
        name="join",
    )(kv, *came, bias)
    x_line = (move(x, far_x), move(y, across_y), x)
    y_line = (move(y, far_y), move(x, partner), y)

    heads = width // HD
    work = heads * side * 3 * side
    half = shape((side, width), bf)

    def attend(turn, line, *more):
        return pl.pallas_call(
            functools.partial(attend_kernel, turn),
            in_specs=[VMEM] * (5 + len(more)),
            out_specs=[VMEM] * 5,
            scratch_shapes=[pltpu.VMEM((HD, 3 * side), bf)] * 2
            + [pltpu.VMEM((HD, 3 * side), jnp.float32)] * 2,
            out_shape=[
                half,
                shape((heads, side, 3 * side), bf),
                block,
                block,
                shape((2, side, HD), jnp.float32),
            ],
            compiler_params=pltpu.CompilerParams(vmem_limit_bytes=32 * 2**20),
            cost_estimate=pl.CostEstimate(
                flops=10 * work * HD, bytes_accessed=6 * side * width, transcendentals=work
            ),
            name="attend",
        )(qg, *line, bias, *more)

    attn_x, ds_x, for_far_x, for_partner, own_x = attend(0, x_line)
    more = move(for_partner, partner, back=True)
    from_far_x = move(for_far_x, far_x, back=True)
    attn_y, ds_y, for_far_y, for_partner, own_y = attend(1, y_line, more)
    terms = (
        (own_x, from_far_x, move(for_partner, partner, back=True)),
        (own_y, move(for_far_y, far_y, back=True)),
    )
    dq_x, dq_y = pl.pallas_call(
        query_kernel,
        out_shape=[half, half],
        in_specs=[VMEM] * 8,
        out_specs=[VMEM] * 2,
        compiler_params=pltpu.CompilerParams(vmem_limit_bytes=16 * 2**20),
        cost_estimate=pl.CostEstimate(
            flops=4 * work * HD, bytes_accessed=4 * work, transcendentals=0
        ),
        name="query",
    )(ds_x, *x_line, ds_y, *y_line)

    pieces = pl.pallas_call(
        functools.partial(total_kernel, groups),
        out_shape=[piece] * groups,
        in_specs=[VMEM] * 5,
        out_specs=[VMEM] * groups,
        compiler_params=SMALL,
        name="total",
    )(*terms[0], *terms[1])
    returned = [pieces[0], *exchange(pieces[1:])]
    attn_out, q_grad, filled = pl.pallas_call(
        fill_kernel,
        out_shape=[shape(queries.shape, bf)] * 2 + [shape((8, HD), jnp.float32)],
        in_specs=[VMEM] * 4 + [ANY],
        out_specs=[HBM, HBM, VMEM],
        scratch_shapes=[pltpu.SemaphoreType.DMA((4,))],
        compiler_params=SMALL,
        cost_estimate=pl.CostEstimate(
            flops=0, bytes_accessed=16 * side * width, transcendentals=0
        ),
        name="fill",
    )(attn_x, attn_y, dq_x, dq_y, returned[1])
    k_grad, v_grad = pl.pallas_call(
        functools.partial(place_kernel, groups),
        out_shape=[shape(keys.shape, bf)] * 2,
        in_specs=[VMEM] * groups + [ANY],
        out_specs=[VMEM] * 2,
        compiler_params=SMALL,
        name="place",
    )(*returned, filled)
    return (attn_out, q_grad, k_grad, v_grad)


def solution(mesh):
    heads, tokens = P(None, "cp", None, "tp"), P(None, "cp", "tp", None)
    return jax.shard_map(
        local,
        mesh=mesh,
        in_specs=(heads, tokens, tokens, heads, P()),
        out_specs=(heads, heads, tokens, tokens),
        check_vma=False,
    )
```
